32 devices in a mesh: pb: 2 (over y), ka: 4 (over x, core), ha: 4 (over z).
Axes of the slice: x: 2, y: 2, z: 4, core: 2. Of those that a mesh axis runs over, the one named last changes fastest.
Arguments:
- queries: bfloat16 [768, 4096], P(('pb', 'ka'), 'ha'), may hold values from -200 to 200
- latents: bfloat16 [768, 8, 128], P(('ka', 'pb'), 'ha'), may hold values from -6 to 6
- key_up: bfloat16 [8, 64, 128], P('ha'), may hold values from -1.5 to 1.5
- value_up: bfloat16 [8, 64, 128], P('ha'), may hold values from -0.75 to 0.75
- documents: int32 [768], replicated, may hold values from 0 to 3, as said below
Outputs:
- attended: bfloat16 [768, 4096], P(('pb', 'ka'), 'ha')
The draws below stay inside these ranges and needn't reach their ends.
Inputs may be any that keep to these rules, and one draw needn't show every extreme that they name: `documents`: ids never fall along the prompt; one document holds exactly 384 positions and none holds more.
All inputs are finite; a program needn't handle non-finite values.
Results may differ from the reference program's by a relative error of at most 0.009.
Values may be sent and summed in bfloat16 or wider, within the bound.
A program may use at most 128 MiB of HBM per device.

```python
import jax
import jax.numpy as jnp
from jax import lax

HEADS = 32
KV_HEADS = 8
HEAD_DIM = 128
RANK = 64
TOKENS = 768


def shared_latents(key):
    sub_key = jax.random.fold_in(key, 101)
    return jnp.clip(jax.random.normal(sub_key, (TOKENS, KV_HEADS, 2 * RANK), jnp.float32), -6.0, 6.0)


def shared_key_up(key):
    sub_key = jax.random.fold_in(key, 102)
    return jnp.clip(jax.random.normal(sub_key, (KV_HEADS, RANK, HEAD_DIM), jnp.float32), -6.0, 6.0) * RANK ** (-0.5)


def draw_queries(key, part):
    base_key = jax.random.fold_in(key, 7)
    values_out = jnp.clip(jax.random.normal(base_key, (TOKENS, HEADS * HEAD_DIM), jnp.float32), -6.0, 6.0)
    return values_out.astype(jnp.bfloat16)


def draw_latents(key, part):
    return shared_latents(key).astype(jnp.bfloat16)


def draw_key_up(key, part):
    return shared_key_up(key).astype(jnp.bfloat16)


def draw_documents(key, part):
    sub_key = jax.random.fold_in(key, 103)
    slot_key, first_key, second_key = jax.random.split(sub_key, 3)
    half_len = TOKENS // 2
    slot = jax.random.randint(slot_key, (), 0, 4)
    first_cut = jax.random.randint(first_key, (), 1, half_len)
    second_cut = jax.random.randint(second_key, (), 1, half_len)
    lower_cut = jnp.minimum(first_cut, second_cut)
    upper_cut = jnp.maximum(first_cut, second_cut)
    shorter = jnp.stack([lower_cut, upper_cut - lower_cut, half_len - upper_cut])
    places = jnp.arange(4, dtype=jnp.int32)
    short_index = jnp.clip(places - (places > slot).astype(jnp.int32), 0, 2)
    lengths = jnp.where(places == slot, half_len, shorter[short_index])
    ends = jnp.cumsum(lengths)
    positions = jnp.arange(TOKENS, dtype=jnp.int32)
    return jnp.sum((positions[:, None] >= ends[None, :3]).astype(jnp.int32), axis=1)


def level_of(rng, extent, pieces, low, high):
    def one(position, shards_of):
        steps = jax.random.uniform(jax.random.fold_in(jax.random.fold_in(rng, 6), position), (shards_of,), jnp.float32, low / len(pieces), high / len(pieces))
        return jnp.repeat(jnp.exp(steps), extent[position] // shards_of).reshape((-1,) + (1,) * (len(extent) - position - 1))

    factor_of = one(*pieces[0])
    for cut in pieces[1:]:
        factor_of = factor_of * one(*cut)
    return factor_of


def scatter_about(key, dims, scale, most, cuts=(), kind=jnp.bfloat16):
    array = scale * jax.random.normal(key, dims, jnp.float32)
    if cuts:
        array = array * level_of(key, dims, cuts, -0.22, 0.18)
    return jnp.clip(array, -most, most).astype(kind)


def setup_inputs(seed: int = 0) -> dict:
    seeds = jax.random.split(jax.random.key(seed), 6)
    queries = draw_queries(jax.random.fold_in(seeds[5], 71), 0)
    latents = draw_latents(jax.random.fold_in(seeds[5], 71), 0)
    key_up = draw_key_up(jax.random.fold_in(seeds[5], 71), 0)
    value_up = scatter_about(seeds[3], (KV_HEADS, RANK, HEAD_DIM), RANK ** -0.5, 0.75, ((0, 4),))
    documents = draw_documents(jax.random.fold_in(seeds[5], 71), 0)
    return {"queries": queries, "latents": latents, "key_up": key_up, "value_up": value_up, "documents": documents}


NEG = -1e30


def frequencies(width):
    steps_half = jnp.arange(width // 2, dtype=jnp.float32)
    base_freq = 500000.0 ** (-2.0 * steps_half / width)
    wavelength = 2.0 * jnp.pi / base_freq
    smooth = (8192.0 / wavelength - 1.0) / 3.0
    blended = (1.0 - smooth) * base_freq / 8.0 + smooth * base_freq
    return jnp.where(wavelength < 2048.0, base_freq, jnp.where(wavelength > 8192.0, base_freq / 8.0, blended))


def rotate(values_in, positions):
    width = values_in.shape[-1]
    angles = positions.astype(jnp.float32)[:, None] * frequencies(width)[None, :]
    cosine = jnp.cos(angles)[:, None, :]
    sine = jnp.sin(angles)[:, None, :]
    first_half = values_in[..., : width // 2]
    second_half = values_in[..., width // 2:]
    return jnp.concatenate([first_half * cosine - second_half * sine, second_half * cosine + first_half * sine], axis=-1)


def reference(queries, latents, key_up, value_up, documents):
    group = HEADS // KV_HEADS
    positions = jnp.arange(TOKENS, dtype=jnp.int32)
    key_full = jnp.einsum("tgr,gre->tge", latents[:, :, :RANK].astype(jnp.float32), key_up.astype(jnp.float32))
    keys = rotate(key_full, positions).astype(jnp.bfloat16)
    values = jnp.einsum("tgr,gre->tge", latents[:, :, RANK:].astype(jnp.float32), value_up.astype(jnp.float32)).astype(jnp.bfloat16)
    block_rows = TOKENS // 16
    scale = HEAD_DIM ** -0.5
    outputs = []
    for block_id in range(16):
        begin = block_id * block_rows
        finish = begin + block_rows
        shaped = queries[begin:finish].astype(jnp.float32).reshape(block_rows, KV_HEADS, group, HEAD_DIM)
        query_pos = positions[begin:finish]
        key_pos = positions[:finish]
        visible = (key_pos[None, :] <= query_pos[:, None]) & (documents[:finish][None, :] == documents[begin:finish][:, None])

        def per_head(operands):
            head_queries, head_keys, head_values = operands
            scores = jnp.einsum("pqd,td->qpt", head_queries, head_keys.astype(jnp.float32)) * scale
            masked = jnp.where(visible[None], scores, NEG)
            row_max = jnp.max(masked, axis=-1, keepdims=True)
            weights = jnp.where(visible[None], jnp.exp(masked - row_max), 0.0)
            rounded = lax.optimization_barrier(weights.astype(jnp.bfloat16)).astype(jnp.float32)
            weighted = jnp.einsum("qpt,td->pqd", rounded, head_values.astype(jnp.float32))
            totals = jnp.transpose(jnp.sum(weights, axis=-1), (1, 0))
            return weighted / totals[..., None]

        operands = (jnp.transpose(shaped, (1, 0, 2, 3)), jnp.transpose(keys[:finish], (1, 0, 2)), jnp.transpose(values[:finish], (1, 0, 2)))
        result = lax.map(per_head, operands)
        result = jnp.transpose(result, (1, 0, 2, 3)).reshape(block_rows, HEADS * HEAD_DIM)
        outputs.append(result.astype(jnp.bfloat16))
    return jnp.concatenate(outputs, axis=0)
```

```python
import functools
import math

import jax
import jax.numpy as jnp
import numpy as np
from jax import lax
from jax.experimental import pallas as pl
from jax.experimental.pallas import tpu as pltpu
from jax.sharding import PartitionSpec as P

NEG = -1e30
MESH = pl.DeviceIdType.MESH


def rotary_tables(rows, blocks, width):
    half = np.arange(width // 2, dtype=np.float64)
    base = 500000.0 ** (-2.0 * half / width)
    wave = 2.0 * np.pi / base
    smooth = (8192.0 / wave - 1.0) / 3.0
    blended = (1.0 - smooth) * base / 8.0 + smooth * base
    freq = np.where(wave < 2048.0, base, np.where(wave > 8192.0, base / 8.0, blended))
    freq = np.concatenate([freq, freq])
    inner = np.arange(rows)[:, None] * freq
    outer = (np.arange(blocks) * rows)[:, None] * freq
    return np.concatenate(
        [np.cos(inner), np.sin(inner), np.cos(outer), np.sin(outer)], axis=0
    ).astype(np.float32)


def each(count, body):
    if count <= 8:
        for index in range(count):
            body(index)
    else:
        lax.fori_loop(0, count, lambda index, _: (body(index), 0)[1], 0)


def kernel(
    plan,
    q_hbm,
    lat_hbm,
    key_up_hbm,
    value_up_hbm,
    docs_hbm,
    table_hbm,
    out_hbm,
    q_buf,
    lat_buf,
    up_buf,
    docs_buf,
    table_buf,
    stage,
    window,
    up_all,
    keys,
    values,
    out_buf,
    row_max,
    total,
    in_sem,
    out_sem,
    send_sem,
    recv_sem,
):
    rows, blocks, back, span, kv, group, width, rank, npb, nka = plan
    slots = back + 1
    pb, ka = lax.axis_index("pb"), lax.axis_index("ka")
    mine_q = pb * nka + ka
    mine_l = ka * npb + pb
    barrier = pltpu.get_barrier_semaphore()

    def greet(slot):
        source = mine_q - back + slot

        @pl.when((source >= 0) & (source != mine_l))
        def _():
            pl.semaphore_signal(
                barrier,
                inc=1,
                device_id={"pb": lax.rem(source, npb), "ka": lax.div(source, npb)},
                device_id_type=MESH,
            )

    each(slots, greet)

    loads = [
        pltpu.make_async_copy(lat_hbm, lat_buf, in_sem.at[0]),
        pltpu.make_async_copy(key_up_hbm, up_buf.at[0], in_sem.at[1]),
        pltpu.make_async_copy(value_up_hbm, up_buf.at[1], in_sem.at[2]),
        pltpu.make_async_copy(docs_hbm, docs_buf, in_sem.at[3]),
        pltpu.make_async_copy(table_hbm, table_buf, in_sem.at[4]),
        pltpu.make_async_copy(q_hbm, q_buf, in_sem.at[5]),
    ]
    for load in loads:
        load.start()

    def clear(slot):
        @pl.when(mine_q - back + slot < 0)
        def _():
            window[slot] = jnp.zeros(window.shape[1:], window.dtype)

    each(slots, clear)

    loads[0].wait()
    place = lax.broadcasted_iota(jnp.int32, (kv * rows, kv * rows), 0)
    col = lax.broadcasted_iota(jnp.int32, (kv * rows, kv * rows), 1)
    pick = jnp.zeros((kv * rows, kv * rows), jnp.float32)
    for g in range(kv):
        here = (place >= g * rows) & (place < (g + 1) * rows)
        pick = jnp.where(here & (col == (place - g * rows) * kv + g), 1.0, pick)
    stage[...] = jnp.dot(
        pick.astype(jnp.bfloat16), lat_buf[...], preferred_element_type=jnp.float32
    ).astype(jnp.bfloat16)

    last = jnp.minimum(blocks - 1, mine_l + back)
    own = ((mine_q >= mine_l) & (mine_q <= last)).astype(jnp.int32)
    partners = last - mine_l + 1 - own

    @pl.when(partners > 0)
    def _():
        pl.semaphore_wait(barrier, partners)

    def copy_to(step):
        target = mine_l + step
        return pltpu.make_async_remote_copy(
            src_ref=stage,
            dst_ref=window.at[back - step],
            send_sem=send_sem.at[step],
            recv_sem=recv_sem.at[back - step],
            device_id={"pb": lax.div(target, nka), "ka": lax.rem(target, nka)},
            device_id_type=MESH,
        )

    def send(step):
        target = mine_l + step

        @pl.when((target < blocks) & (target != mine_q))
        def _():
            copy_to(step).start()

        @pl.when(target == mine_q)
        def _():
            window[back - step] = stage[...]

    each(slots, send)

    loads[1].wait()
    loads[2].wait()
    up_all[...] = jnp.zeros(up_all.shape, up_all.dtype)
    for g in range(kv):
        up_all[g, :rank, :width] = up_buf[0, g]
        up_all[g, rank:, width:] = up_buf[1, g]
    loads[3].wait()
    docs = docs_buf[...]
    query_at = mine_q * rows + lax.broadcasted_iota(jnp.int32, (rows, 1), 0)
    query_at = query_at.astype(jnp.float32)
    begin = jnp.zeros((rows, 1), jnp.float32)
    for doc in range(3):
        cut = jnp.sum(jnp.where(docs <= doc, 1.0, 0.0), axis=0, keepdims=True)
        cut = jnp.sum(cut, axis=1, keepdims=True)
        begin = jnp.maximum(begin, jnp.where(cut <= query_at, cut, 0.0))

    loads[4].wait()
    cos_row, sin_row = table_buf[:rows], table_buf[rows : 2 * rows]
    lane = lax.broadcasted_iota(jnp.int32, (1, width), 1)
    sign = jnp.where(lane < width // 2, -1.0, 1.0)

    def rebuild(slot):
        source = mine_q - back + slot

        @pl.when((source >= 0) & (source != mine_l))
        def _():
            pltpu.make_async_copy(stage, window.at[slot], recv_sem.at[slot]).wait()

        first = jnp.maximum(source, 0)
        cos_block = table_buf[pl.ds(2 * rows + first, 1)]
        sin_block = table_buf[pl.ds(2 * rows + blocks + first, 1)]
        cosine = cos_row * cos_block - sin_row * sin_block
        sine = (sin_row * cos_block + cos_row * sin_block) * sign
        at = slot * rows if isinstance(slot, int) else pl.multiple_of(slot * rows, rows)
        for g in range(kv):
            both = jnp.dot(
                window[slot, g * rows : (g + 1) * rows],
                up_all[g],
                preferred_element_type=jnp.float32,
            )
            key = both[:, :width]
            key = key * cosine + pltpu.roll(key, width // 2, 1) * sine
            keys[g, pl.ds(at, rows)] = key.astype(jnp.bfloat16)
            values[g, pl.ds(at, rows), :width] = both[:, width:].astype(jnp.bfloat16)
            values[g, pl.ds(at, rows), width:] = jnp.ones((rows, width), jnp.bfloat16)

    each(slots, rebuild)

    factor = math.log2(math.e) * width ** (-0.5)
    reach = span * rows
    loads[5].wait()

    def attend(chunk):
        at = chunk * reach if isinstance(chunk, int) else pl.multiple_of(chunk * reach, reach)
        key_at = (mine_q - back + chunk * span) * rows
        key_at = key_at + lax.broadcasted_iota(jnp.int32, (1, reach), 1)
        key_at = key_at.astype(jnp.float32)
        bias = jnp.where((key_at >= begin) & (key_at <= query_at), 0.0, NEG)
        for g in range(kv):
            for h in range(g * group, (g + 1) * group):
                scores = lax.dot_general(
                    q_buf[:, h * width : (h + 1) * width],
                    keys[g, pl.ds(at, reach)],
                    (((1,), (1,)), ((), ())),
                    preferred_element_type=jnp.float32,
                )
                scores = scores + bias
                top = jnp.max(scores, axis=1, keepdims=True)
                if span < slots:
                    before = row_max[h]
                    top = jnp.maximum(top, before)
                    row_max[h] = top
                    scale = jnp.exp2((before - top) * factor)
                weights = jnp.exp2((scores - top) * factor).astype(jnp.bfloat16)
                part = jnp.dot(
                    weights, values[g, pl.ds(at, reach)], preferred_element_type=jnp.float32
                )
                if span < slots:
                    total[h] = total[h] * scale + part
                else:
                    out_buf[:, h * width : (h + 1) * width] = (
                        part[:, :width] / part[:, width:]
                    ).astype(jnp.bfloat16)

    if span < slots:
        row_max[...] = jnp.full(row_max.shape, NEG, jnp.float32)
        total[...] = jnp.zeros(total.shape, jnp.float32)
        lax.fori_loop(0, slots // span, lambda c, _: (attend(c), 0)[1], 0)
        for h in range(kv * group):
            out_buf[:, h * width : (h + 1) * width] = (
                total[h, :, :width] / total[h, :, width:]
            ).astype(jnp.bfloat16)
    else:
        attend(0)
    done = pltpu.make_async_copy(out_buf, out_hbm, out_sem)
    done.start()

    def drain(step):
        target = mine_l + step

        @pl.when((target < blocks) & (target != mine_q))
        def _():
            copy_to(step).wait_send()

    each(slots, drain)
    done.wait()


def shards(queries, latents, key_up, value_up, documents):
    rows = queries.shape[0]
    kv, rank, width = key_up.shape
    heads = queries.shape[1] // width
    npb, nka = lax.axis_size("pb"), lax.axis_size("ka")
    blocks = npb * nka
    tokens = documents.shape[0]
    back = -(-(tokens // 2 - 1) // rows)
    slots = back + 1
    span = max(d for d in range(1, 9) if slots % d == 0)
    many = span < slots
    table = jnp.asarray(rotary_tables(rows, blocks, width))
    plan = (rows, blocks, back, span, kv, heads // kv, width, rank, npb, nka)
    bf16, f32 = jnp.bfloat16, jnp.float32
    return pl.pallas_call(
        functools.partial(kernel, plan),
        out_shape=jax.ShapeDtypeStruct(queries.shape, bf16),
        in_specs=[pl.BlockSpec(memory_space=pl.ANY)] * 6,
        out_specs=pl.BlockSpec(memory_space=pl.ANY),
        scratch_shapes=[
            pltpu.VMEM(queries.shape, bf16),
            pltpu.VMEM((rows * kv, 2 * rank), bf16),
            pltpu.VMEM((2, kv, rank, width), bf16),
            pltpu.VMEM((tokens // 128, 128), jnp.int32),
            pltpu.VMEM(table.shape, f32),
            pltpu.VMEM((rows * kv, 2 * rank), bf16),
            pltpu.VMEM((slots, rows * kv, 2 * rank), bf16),
            pltpu.VMEM((kv, 2 * rank, 2 * width), bf16),
            pltpu.VMEM((kv, slots * rows, width), bf16),
            pltpu.VMEM((kv, slots * rows, 2 * width), bf16),
            pltpu.VMEM(queries.shape, bf16),
            pltpu.VMEM((heads if many else 1, rows, 1), f32),
            pltpu.VMEM((heads if many else 1, rows, 2 * width), f32),
            pltpu.SemaphoreType.DMA((6,)),
            pltpu.SemaphoreType.DMA,
            pltpu.SemaphoreType.DMA((slots,)),
            pltpu.SemaphoreType.DMA((slots,)),
        ],
        compiler_params=pltpu.CompilerParams(
            collective_id=0, has_side_effects=True, vmem_limit_bytes=40 * 2**20
        ),
    )(
        queries,
        latents.reshape(rows * kv, 2 * rank),
        key_up,
        value_up,
        documents.reshape(tokens // 128, 128),
        table,
    )


def solution(mesh):
    placed = (
        P(("pb", "ka"), "ha"),
        P(("ka", "pb"), "ha", None),
        P("ha", None, None),
        P("ha", None, None),
        P(),
    )
    return jax.shard_map(
        shards, mesh=mesh, in_specs=placed, out_specs=P(("pb", "ka"), "ha"), check_vma=False
    )
```

```python
import functools
import math

import jax
import jax.numpy as jnp
import numpy as np
from jax import lax
from jax.experimental import pallas as pl
from jax.experimental.pallas import tpu as pltpu
from jax.sharding import PartitionSpec as P

NEG = -1e30
MESH = pl.DeviceIdType.MESH


def rotary_tables(rows, blocks, width):
    half = np.arange(width // 2, dtype=np.float64)
    base = 500000.0 ** (-2.0 * half / width)
    wave = 2.0 * np.pi / base
    smooth = (8192.0 / wave - 1.0) / 3.0
    blended = (1.0 - smooth) * base / 8.0 + smooth * base
    freq = np.where(wave < 2048.0, base, np.where(wave > 8192.0, base / 8.0, blended))
    freq = np.concatenate([freq, freq])
    inner = np.arange(rows)[:, None] * freq
    outer = (np.arange(blocks) * rows)[:, None] * freq
    return np.concatenate(
        [np.cos(inner), np.sin(inner), np.cos(outer), np.sin(outer)], axis=0
    ).astype(np.float32)


def each(count, body):
    if count <= 8:
        for index in range(count):
            body(index)
    else:
        lax.fori_loop(0, count, lambda index, _: (body(index), 0)[1], 0)


def kernel(
    plan,
    q_hbm,
    lat_hbm,
    key_up_hbm,
    value_up_hbm,
    docs_hbm,
    table_hbm,
    out_hbm,
    q_buf,
    lat_buf,
    up_buf,
    docs_buf,
    table_buf,
    stage,
    window,
    up_all,
    keys,
    values,
    out_buf,
    row_max,
    total,
    in_sem,
    out_sem,
    send_sem,
    recv_sem,
):
    rows, blocks, back, span, kv, group, width, rank, npb, nka = plan
    slots = back + 1
    pb, ka = lax.axis_index("pb"), lax.axis_index("ka")
    mine_q = pb * nka + ka
    mine_l = ka * npb + pb
    barrier = pltpu.get_barrier_semaphore()

    def greet(slot):
        source = mine_q - back + slot

        @pl.when((source >= 0) & (source != mine_l))
        def _():
            pl.semaphore_signal(
                barrier,
                inc=1,
                device_id={"pb": lax.rem(source, npb), "ka": lax.div(source, npb)},
                device_id_type=MESH,
            )

    each(slots, greet)

    loads = [
        pltpu.make_async_copy(lat_hbm, lat_buf, in_sem.at[0]),
        pltpu.make_async_copy(key_up_hbm, up_buf.at[0], in_sem.at[1]),
        pltpu.make_async_copy(value_up_hbm, up_buf.at[1], in_sem.at[2]),
        pltpu.make_async_copy(docs_hbm, docs_buf, in_sem.at[3]),
        pltpu.make_async_copy(table_hbm, table_buf, in_sem.at[4]),
        pltpu.make_async_copy(q_hbm, q_buf, in_sem.at[5]),
    ]
    for load in loads:
        load.start()

    def clear(slot):
        @pl.when(mine_q - back + slot < 0)
        def _():
            window[slot] = jnp.zeros(window.shape[1:], window.dtype)

    each(slots, clear)

    loads[0].wait()
    place = lax.broadcasted_iota(jnp.int32, (kv * rows, kv * rows), 0)
    col = lax.broadcasted_iota(jnp.int32, (kv * rows, kv * rows), 1)
    pick = jnp.zeros((kv * rows, kv * rows), jnp.float32)
    for g in range(kv):
        here = (place >= g * rows) & (place < (g + 1) * rows)
        pick = jnp.where(here & (col == (place - g * rows) * kv + g), 1.0, pick)
    stage[...] = jnp.dot(
        pick.astype(jnp.bfloat16), lat_buf[...], preferred_element_type=jnp.float32
    ).astype(jnp.bfloat16)

    last = jnp.minimum(blocks - 1, mine_l + back)
    own = ((mine_q >= mine_l) & (mine_q <= last)).astype(jnp.int32)
    partners = last - mine_l + 1 - own

    @pl.when(partners > 0)
    def _():
        pl.semaphore_wait(barrier, partners)

    def copy_to(step):
        target = mine_l + step
        return pltpu.make_async_remote_copy(
            src_ref=stage,
            dst_ref=window.at[back - step],
            send_sem=send_sem.at[step],
            recv_sem=recv_sem.at[back - step],
            device_id={"pb": lax.div(target, nka), "ka": lax.rem(target, nka)},
            device_id_type=MESH,
        )

    def send(step):
        target = mine_l + step

        @pl.when((target < blocks) & (target != mine_q))
        def _():
            copy_to(step).start()

        @pl.when(target == mine_q)
        def _():
            window[back - step] = stage[...]

    each(slots, send)

    loads[1].wait()
    loads[2].wait()
    up_all[...] = jnp.zeros(up_all.shape, up_all.dtype)
    for g in range(kv):
        up_all[g, :rank, :width] = up_buf[0, g]
        up_all[g, rank:, width:] = up_buf[1, g]
    loads[3].wait()
    docs = docs_buf[...]
    query_at = mine_q * rows + lax.broadcasted_iota(jnp.int32, (rows, 1), 0)
    query_at = query_at.astype(jnp.float32)
    begin = jnp.zeros((rows, 1), jnp.float32)
    for doc in range(3):
        cut = jnp.sum(jnp.where(docs <= doc, 1.0, 0.0), axis=0, keepdims=True)
        cut = jnp.sum(cut, axis=1, keepdims=True)
        begin = jnp.maximum(begin, jnp.where(cut <= query_at, cut, 0.0))

    loads[4].wait()
    cos_row, sin_row = table_buf[:rows], table_buf[rows : 2 * rows]
    lane = lax.broadcasted_iota(jnp.int32, (1, width), 1)
    sign = jnp.where(lane < width // 2, -1.0, 1.0)

    def rebuild(slot):
        source = mine_q - back + slot

        @pl.when((source >= 0) & (source != mine_l))
        def _():
            pltpu.make_async_copy(stage, window.at[slot], recv_sem.at[slot]).wait()

        first = jnp.maximum(source, 0)
        cos_block = table_buf[pl.ds(2 * rows + first, 1)]
        sin_block = table_buf[pl.ds(2 * rows + blocks + first, 1)]
        cosine = cos_row * cos_block - sin_row * sin_block
        sine = (sin_row * cos_block + cos_row * sin_block) * sign
        at = slot * rows if isinstance(slot, int) else pl.multiple_of(slot * rows, rows)
        for g in range(kv):
            both = jnp.dot(
                window[slot, g * rows : (g + 1) * rows],
                up_all[g],
                preferred_element_type=jnp.float32,
            )
            key = both[:, :width]
            key = key * cosine + pltpu.roll(key, width // 2, 1) * sine
            keys[g, pl.ds(at, rows)] = key.astype(jnp.bfloat16)
            values[g, pl.ds(at, rows), :width] = both[:, width:].astype(jnp.bfloat16)
            values[g, pl.ds(at, rows), width:] = jnp.ones((rows, width), jnp.bfloat16)

    each(slots, rebuild)

    factor = math.log2(math.e) * width ** (-0.5)
    reach = span * rows
    loads[5].wait()

    def attend(chunk):
        at = chunk * reach if isinstance(chunk, int) else pl.multiple_of(chunk * reach, reach)
        key_at = (mine_q - back + chunk * span) * rows
        key_at = key_at + lax.broadcasted_iota(jnp.int32, (1, reach), 1)
        key_at = key_at.astype(jnp.float32)
        bias = jnp.where((key_at >= begin) & (key_at <= query_at), 0.0, NEG)
        for g in range(kv):
            for h in range(g * group, (g + 1) * group):
                scores = lax.dot_general(
                    q_buf[:, h * width : (h + 1) * width],
                    keys[g, pl.ds(at, reach)],
                    (((1,), (1,)), ((), ())),
                    preferred_element_type=jnp.float32,
                )
                scores = scores + bias
                top = jnp.max(scores, axis=1, keepdims=True)
                if span < slots:
                    before = row_max[h]
                    top = jnp.maximum(top, before)
                    row_max[h] = top
                    scale = jnp.exp2((before - top) * factor)
                weights = jnp.exp2((scores - top) * factor).astype(jnp.bfloat16)
                part = jnp.dot(
                    weights, values[g, pl.ds(at, reach)], preferred_element_type=jnp.float32
                )
                if span < slots:
                    total[h] = total[h] * scale + part
                else:
                    out_buf[:, h * width : (h + 1) * width] = (
                        part[:, :width] / part[:, width:]
                    ).astype(jnp.bfloat16)

    if span < slots:
        row_max[...] = jnp.full(row_max.shape, NEG, jnp.float32)
        total[...] = jnp.zeros(total.shape, jnp.float32)
        lax.fori_loop(0, slots // span, lambda c, _: (attend(c), 0)[1], 0)
        for h in range(kv * group):
            out_buf[:, h * width : (h + 1) * width] = (
                total[h, :, :width] / total[h, :, width:]
            ).astype(jnp.bfloat16)
    else:
        attend(0)
    done = pltpu.make_async_copy(out_buf, out_hbm, out_sem)
    done.start()

    def drain(step):
        target = mine_l + step

        @pl.when((target < blocks) & (target != mine_q))
        def _():
            copy_to(step).wait_send()

    each(slots, drain)
    done.wait()


def shards(queries, latents, key_up, value_up, documents):
    rows = queries.shape[0]
    kv, rank, width = key_up.shape
    heads = queries.shape[1] // width
    npb, nka = lax.axis_size("pb"), lax.axis_size("ka")
    blocks = npb * nka
    tokens = documents.shape[0]
    back = -(-(tokens // 2 - 1) // rows)
    slots = back + 1
    span = max(d for d in range(1, 9) if slots % d == 0)
    many = span < slots
    table = jnp.asarray(rotary_tables(rows, blocks, width))
    plan = (rows, blocks, back, span, kv, heads // kv, width, rank, npb, nka)
    bf16, f32 = jnp.bfloat16, jnp.float32
    return pl.pallas_call(
        functools.partial(kernel, plan),
        out_shape=jax.ShapeDtypeStruct(queries.shape, bf16),
        in_specs=[pl.BlockSpec(memory_space=pltpu.HBM)] * 6,
        out_specs=pl.BlockSpec(memory_space=pltpu.HBM),
        scratch_shapes=[
            pltpu.VMEM(queries.shape, bf16),
            pltpu.VMEM((rows * kv, 2 * rank), bf16),
            pltpu.VMEM((2, kv, rank, width), bf16),
            pltpu.VMEM((tokens // 128, 128), jnp.int32),
            pltpu.VMEM(table.shape, f32),
            pltpu.VMEM((rows * kv, 2 * rank), bf16),
            pltpu.VMEM((slots, rows * kv, 2 * rank), bf16),
            pltpu.VMEM((kv, 2 * rank, 2 * width), bf16),
            pltpu.VMEM((kv, slots * rows, width), bf16),
            pltpu.VMEM((kv, slots * rows, 2 * width), bf16),
            pltpu.VMEM(queries.shape, bf16),
            pltpu.VMEM((heads if many else 1, rows, 1), f32),
            pltpu.VMEM((heads if many else 1, rows, 2 * width), f32),
            pltpu.SemaphoreType.DMA((6,)),
            pltpu.SemaphoreType.DMA,
            pltpu.SemaphoreType.DMA((slots,)),
            pltpu.SemaphoreType.DMA((slots,)),
        ],
        compiler_params=pltpu.CompilerParams(
            collective_id=0, has_side_effects=True, vmem_limit_bytes=63 * 2**20
        ),
    )(
        queries,
        latents.reshape(rows * kv, 2 * rank),
        key_up,
        value_up,
        documents.reshape(tokens // 128, 128),
        table,
    )


def solution(mesh):
    placed = (
        P(("pb", "ka"), "ha"),
        P(("ka", "pb"), "ha", None),
        P("ha", None, None),
        P("ha", None, None),
        P(),
    )
    return jax.shard_map(
        shards, mesh=mesh, in_specs=placed, out_specs=P(("pb", "ka"), "ha"), check_vma=False
    )
```

```python
import functools
import math

import jax
import jax.numpy as jnp
import numpy as np
from jax import lax
from jax.experimental import pallas as pl
from jax.experimental.pallas import tpu as pltpu
from jax.sharding import PartitionSpec as P

NEG = -1e30
MESH = pl.DeviceIdType.MESH


def rotary_tables(rows, blocks, width):
    half = np.arange(width // 2, dtype=np.float64)
    base = 500000.0 ** (-2.0 * half / width)
    wave = 2.0 * np.pi / base
    smooth = (8192.0 / wave - 1.0) / 3.0
    blended = (1.0 - smooth) * base / 8.0 + smooth * base
    freq = np.where(wave < 2048.0, base, np.where(wave > 8192.0, base / 8.0, blended))
    freq = np.concatenate([freq, freq])
    inner = np.arange(rows)[:, None] * freq
    outer = (np.arange(blocks) * rows)[:, None] * freq
    return np.concatenate(
        [np.cos(inner), np.sin(inner), np.cos(outer), np.sin(outer)], axis=0
    ).astype(np.float32)


def each(count, body):
    if count <= 8:
        for index in range(count):
            body(index)
    else:
        lax.fori_loop(0, count, lambda index, _: (body(index), 0)[1], 0)


def kernel(
    plan,
    q_hbm,
    lat_hbm,
    key_up_hbm,
    value_up_hbm,
    docs_hbm,
    table_hbm,
    out_ref,
    q_buf,
    lat_buf,
    up_buf,
    docs_buf,
    table_buf,
    stage,
    window,
    up_all,
    keys,
    values,
    row_max,
    total,
    in_sem,
    send_sem,
    recv_sem,
):
    rows, blocks, back, span, kv, group, width, rank, npb, nka = plan
    slots = back + 1
    pb, ka = lax.axis_index("pb"), lax.axis_index("ka")
    mine_q = pb * nka + ka
    mine_l = ka * npb + pb
    barrier = pltpu.get_barrier_semaphore()

    def greet(slot):
        source = mine_q - back + slot

        @pl.when((source >= 0) & (source != mine_l))
        def _():
            pl.semaphore_signal(
                barrier,
                inc=1,
                device_id={"pb": lax.rem(source, npb), "ka": lax.div(source, npb)},
                device_id_type=MESH,
            )

    each(slots, greet)

    loads = [
        pltpu.make_async_copy(lat_hbm, lat_buf, in_sem.at[0]),
        pltpu.make_async_copy(key_up_hbm, up_buf.at[0], in_sem.at[1]),
        pltpu.make_async_copy(value_up_hbm, up_buf.at[1], in_sem.at[2]),
        pltpu.make_async_copy(docs_hbm, docs_buf, in_sem.at[3]),
        pltpu.make_async_copy(table_hbm, table_buf, in_sem.at[4]),
        pltpu.make_async_copy(q_hbm, q_buf, in_sem.at[5]),
    ]
    for load in loads:
        load.start()

    def clear(slot):
        @pl.when(mine_q - back + slot < 0)
        def _():
            window[slot] = jnp.zeros(window.shape[1:], window.dtype)

    each(slots, clear)

    loads[0].wait()
    place = lax.broadcasted_iota(jnp.int32, (kv * rows, kv * rows), 0)
    col = lax.broadcasted_iota(jnp.int32, (kv * rows, kv * rows), 1)
    pick = jnp.zeros((kv * rows, kv * rows), jnp.float32)
    for g in range(kv):
        here = (place >= g * rows) & (place < (g + 1) * rows)
        pick = jnp.where(here & (col == (place - g * rows) * kv + g), 1.0, pick)
    stage[...] = jnp.dot(
        pick.astype(jnp.bfloat16), lat_buf[...], preferred_element_type=jnp.float32
    ).astype(jnp.bfloat16)

    last = jnp.minimum(blocks - 1, mine_l + back)
    own = ((mine_q >= mine_l) & (mine_q <= last)).astype(jnp.int32)
    partners = last - mine_l + 1 - own

    @pl.when(partners > 0)
    def _():
        pl.semaphore_wait(barrier, partners)

    def copy_to(step):
        target = mine_l + step
        return pltpu.make_async_remote_copy(
            src_ref=stage,
            dst_ref=window.at[back - step],
            send_sem=send_sem.at[step],
            recv_sem=recv_sem.at[back - step],
            device_id={"pb": lax.div(target, nka), "ka": lax.rem(target, nka)},
            device_id_type=MESH,
        )

    def send(step):
        target = mine_l + step

        @pl.when((target < blocks) & (target != mine_q))
        def _():
            copy_to(step).start()

        @pl.when(target == mine_q)
        def _():
            window[back - step] = stage[...]

    each(slots, send)

    loads[1].wait()
    loads[2].wait()
    up_all[...] = jnp.zeros(up_all.shape, up_all.dtype)
    for g in range(kv):
        up_all[g, :rank, :width] = up_buf[0, g]
        up_all[g, rank:, width:] = up_buf[1, g]
    loads[3].wait()
    docs = docs_buf[...]
    query_at = mine_q * rows + lax.broadcasted_iota(jnp.int32, (rows, 1), 0)
    query_at = query_at.astype(jnp.float32)
    begin = jnp.zeros((rows, 1), jnp.float32)
    for doc in range(3):
        cut = jnp.sum(jnp.where(docs <= doc, 1.0, 0.0), axis=0, keepdims=True)
        cut = jnp.sum(cut, axis=1, keepdims=True)
        begin = jnp.maximum(begin, jnp.where(cut <= query_at, cut, 0.0))

    loads[4].wait()
    cos_row, sin_row = table_buf[:rows], table_buf[rows : 2 * rows]
    lane = lax.broadcasted_iota(jnp.int32, (1, width), 1)
    sign = jnp.where(lane < width // 2, -1.0, 1.0)

    def rebuild(slot):
        source = mine_q - back + slot

        @pl.when((source >= 0) & (source != mine_l))
        def _():
            pltpu.make_async_copy(stage, window.at[slot], recv_sem.at[slot]).wait()

        first = jnp.maximum(source, 0)
        cos_block = table_buf[pl.ds(2 * rows + first, 1)]
        sin_block = table_buf[pl.ds(2 * rows + blocks + first, 1)]
        cosine = cos_row * cos_block - sin_row * sin_block
        sine = (sin_row * cos_block + cos_row * sin_block) * sign
        at = slot * rows if isinstance(slot, int) else pl.multiple_of(slot * rows, rows)
        for g in range(kv):
            both = jnp.dot(
                window[slot, g * rows : (g + 1) * rows],
                up_all[g],
                preferred_element_type=jnp.float32,
            )
            key = both[:, :width]
            key = key * cosine + pltpu.roll(key, width // 2, 1) * sine
            keys[g, pl.ds(at, rows)] = key.astype(jnp.bfloat16)
            values[g, pl.ds(at, rows), :width] = both[:, width:].astype(jnp.bfloat16)
            values[g, pl.ds(at, rows), width:] = jnp.ones((rows, width), jnp.bfloat16)

    each(slots, rebuild)

    factor = math.log2(math.e) * width ** (-0.5)
    reach = span * rows
    loads[5].wait()

    def attend(chunk):
        at = chunk * reach if isinstance(chunk, int) else pl.multiple_of(chunk * reach, reach)
        key_at = (mine_q - back + chunk * span) * rows
        key_at = key_at + lax.broadcasted_iota(jnp.int32, (1, reach), 1)
        key_at = key_at.astype(jnp.float32)
        bias = jnp.where((key_at >= begin) & (key_at <= query_at), 0.0, NEG)
        bias = jnp.concatenate([bias] * group, axis=0)
        for g in range(kv):
            heads = range(g * group, (g + 1) * group)
            stacked = jnp.concatenate([q_buf[:, h * width : (h + 1) * width] for h in heads])
            scores = lax.dot_general(
                stacked,
                keys[g, pl.ds(at, reach)],
                (((1,), (1,)), ((), ())),
                preferred_element_type=jnp.float32,
            )
            scores = scores + bias
            top = jnp.max(scores, axis=1, keepdims=True)
            if span < slots:
                before = row_max[g]
                top = jnp.maximum(top, before)
                row_max[g] = top
                scale = jnp.exp2((before - top) * factor)
            weights = jnp.exp2((scores - top) * factor).astype(jnp.bfloat16)
            part = jnp.dot(
                weights, values[g, pl.ds(at, reach)], preferred_element_type=jnp.float32
            )
            if span < slots:
                total[g] = total[g] * scale + part
            else:
                write(g, part)

    def write(g, part):
        ratio = (part[:, :width] / part[:, width:]).astype(jnp.bfloat16)
        for i in range(group):
            h = g * group + i
            out_ref[:, h * width : (h + 1) * width] = ratio[i * rows : (i + 1) * rows]

    if span < slots:
        row_max[...] = jnp.full(row_max.shape, NEG, jnp.float32)
        total[...] = jnp.zeros(total.shape, jnp.float32)
        lax.fori_loop(0, slots // span, lambda c, _: (attend(c), 0)[1], 0)
        for g in range(kv):
            write(g, total[g])
    else:
        attend(0)

    def drain(step):
        target = mine_l + step

        @pl.when((target < blocks) & (target != mine_q))
        def _():
            copy_to(step).wait_send()

    each(slots, drain)


def shards(queries, latents, key_up, value_up, documents):
    rows = queries.shape[0]
    kv, rank, width = key_up.shape
    heads = queries.shape[1] // width
    npb, nka = lax.axis_size("pb"), lax.axis_size("ka")
    blocks = npb * nka
    tokens = documents.shape[0]
    back = -(-(tokens // 2 - 1) // rows)
    slots = back + 1
    span = max(d for d in range(1, 9) if slots % d == 0)
    many = span < slots
    table = jnp.asarray(rotary_tables(rows, blocks, width))
    plan = (rows, blocks, back, span, kv, heads // kv, width, rank, npb, nka)
    bf16, f32 = jnp.bfloat16, jnp.float32
    return pl.pallas_call(
        functools.partial(kernel, plan),
        out_shape=pltpu.VMEM(queries.shape, bf16),
        in_specs=[pl.BlockSpec(memory_space=pltpu.HBM)] * 6,
        out_specs=pl.BlockSpec(memory_space=pltpu.VMEM),
        scratch_shapes=[
            pltpu.VMEM(queries.shape, bf16),
            pltpu.VMEM((rows * kv, 2 * rank), bf16),
            pltpu.VMEM((2, kv, rank, width), bf16),
            pltpu.VMEM((tokens // 128, 128), jnp.int32),
            pltpu.VMEM(table.shape, f32),
            pltpu.VMEM((rows * kv, 2 * rank), bf16),
            pltpu.VMEM((slots, rows * kv, 2 * rank), bf16),
            pltpu.VMEM((kv, 2 * rank, 2 * width), bf16),
            pltpu.VMEM((kv, slots * rows, width), bf16),
            pltpu.VMEM((kv, slots * rows, 2 * width), bf16),
            pltpu.VMEM((kv, heads // kv * rows if many else 8, 1), f32),
            pltpu.VMEM((kv, heads // kv * rows if many else 8, 2 * width), f32),
            pltpu.SemaphoreType.DMA((6,)),
            pltpu.SemaphoreType.DMA((slots,)),
            pltpu.SemaphoreType.DMA((slots,)),
        ],
        compiler_params=pltpu.CompilerParams(
            collective_id=0, has_side_effects=True, vmem_limit_bytes=63 * 2**20
        ),
    )(
        queries,
        latents.reshape(rows * kv, 2 * rank),
        key_up,
        value_up,
        documents.reshape(tokens // 128, 128),
        table,
    )


def solution(mesh):
    placed = (
        P(("pb", "ka"), "ha"),
        P(("ka", "pb"), "ha", None),
        P("ha", None, None),
        P("ha", None, None),
        P(),
    )
    return jax.shard_map(
        shards, mesh=mesh, in_specs=placed, out_specs=P(("pb", "ka"), "ha"), check_vma=False
    )
```

```python
import functools
import math

import jax
import jax.numpy as jnp
import numpy as np
from jax import lax
from jax.experimental import pallas as pl
from jax.experimental.pallas import tpu as pltpu
from jax.sharding import PartitionSpec as P

NEG = -1e30
MESH = pl.DeviceIdType.MESH


def rotary_tables(rows, blocks, width):
    half = np.arange(width // 2, dtype=np.float64)
    base = 500000.0 ** (-2.0 * half / width)
    wave = 2.0 * np.pi / base
    smooth = (8192.0 / wave - 1.0) / 3.0
    blended = (1.0 - smooth) * base / 8.0 + smooth * base
    freq = np.where(wave < 2048.0, base, np.where(wave > 8192.0, base / 8.0, blended))
    freq = np.concatenate([freq, freq])
    inner = np.arange(rows)[:, None] * freq
    outer = (np.arange(blocks) * rows)[:, None] * freq
    return np.concatenate(
        [np.cos(inner), np.sin(inner), np.cos(outer), np.sin(outer)], axis=0
    ).astype(np.float32)


def each(count, body):
    if count <= 8:
        for index in range(count):
            body(index)
    else:
        lax.fori_loop(0, count, lambda index, _: (body(index), 0)[1], 0)


def kernel(
    plan,
    q_hbm,
    lat_hbm,
    key_up_hbm,
    value_up_hbm,
    docs_hbm,
    table_hbm,
    out_ref,
    q_buf,
    up_buf,
    docs_buf,
    table_buf,
    pick,
    cosines,
    sines,
    window,
    up_all,
    keys,
    values,
    row_max,
    total,
    in_sem,
    send_sem,
    recv_sem,
    pass_sem,
    mate_sem,
):
    rows, blocks, back, span, kv, group, width, rank, npb, nka = plan
    slots = back + 1
    half = rows * kv // 2
    pb, ka = lax.axis_index("pb"), lax.axis_index("ka")
    mine_q = pb * nka + ka
    mine_l = ka * npb + pb
    core = lax.rem(ka, 2)
    pair = lax.div(mine_q, 2)
    mate = ka + 1 - 2 * core
    base = 2 * pair - back
    barrier = pltpu.get_barrier_semaphore()

    def greet_at(at_pb, at_ka):
        pl.semaphore_signal(
            barrier, inc=1, device_id={"pb": at_pb, "ka": at_ka}, device_id_type=MESH
        )

    def greet(slot):
        source = base + slot

        @pl.when((source >= 0) & (source != mine_l))
        def _():
            greet_at(lax.rem(source, npb), lax.div(source, npb))

    each(slots + 1, greet)
    mate_l = mate * npb + pb
    mate_apart = (mate_l < base) | (mate_l > 2 * pair + 1)

    @pl.when(mate_apart)
    def _():
        greet_at(pb, mate)

    loads = [
        pltpu.make_async_copy(docs_hbm, docs_buf, in_sem.at[0]),
        pltpu.make_async_copy(table_hbm, table_buf, in_sem.at[1]),
        pltpu.make_async_copy(key_up_hbm, up_buf.at[0], in_sem.at[2]),
        pltpu.make_async_copy(value_up_hbm, up_buf.at[1], in_sem.at[3]),
        pltpu.make_async_copy(q_hbm, q_buf, in_sem.at[4]),
    ]
    for load in loads:
        load.start()

    def part_of(ref, which):
        return ref.at[pl.ds(pl.multiple_of(which * half, half), half)]

    def take_own(slot):
        return pltpu.make_async_copy(
            part_of(lat_hbm, core), part_of(window.at[slot], core), recv_sem.at[slot]
        )

    def keep(slot):
        @pl.when(base + slot == mine_l)
        def _():
            take_own(slot).start()

    each(slots + 1, keep)

    first_pair = lax.div(mine_l, 2)
    last_pair = jnp.minimum(blocks // 2 - 1, lax.div(mine_l + back, 2))
    inside = ((pair >= first_pair) & (pair <= last_pair)).astype(jnp.int32)
    pl.semaphore_wait(barrier, 2 * (last_pair - first_pair + 1) + 1 - 2 * inside)

    def copy_to(step):
        target, side = first_pair + step // 2, step % 2
        slot = mine_l - 2 * target + back
        other = 2 * target + side
        return pltpu.make_async_remote_copy(
            src_ref=lat_hbm.at[pl.ds(side * half, half)],
            dst_ref=window.at[slot, pl.ds(side * half, half)],
            send_sem=send_sem.at[step],
            recv_sem=recv_sem.at[slot],
            device_id={"pb": lax.div(other, nka), "ka": lax.rem(other, nka)},
            device_id_type=MESH,
        )

    reached = 2 * (back // 2 + 1 + back % 2)

    def goes(step):
        target = first_pair + step // 2
        return (target <= last_pair) & (2 * target + step % 2 != mine_q)

    def send(step):
        @pl.when(goes(step))
        def _():
            copy_to(step).start()

    each(reached, send)

    def clear(slot):
        @pl.when(base + slot < 0)
        def _():
            window[slot] = jnp.zeros(window.shape[1:], window.dtype)

    each(slots + 1, clear)
    values[:, :, width:] = jnp.ones((kv, slots * rows, width), jnp.bfloat16)
    up_all[...] = jnp.zeros(up_all.shape, up_all.dtype)
    place = lax.broadcasted_iota(jnp.int32, (kv * rows, kv * rows), 0)
    col = lax.broadcasted_iota(jnp.int32, (kv * rows, kv * rows), 1)
    sort = jnp.zeros((kv * rows, kv * rows), jnp.float32)
    for g in range(kv):
        here = (place >= g * rows) & (place < (g + 1) * rows)
        sort = jnp.where(here & (col == (place - g * rows) * kv + g), 1.0, sort)
    pick[...] = sort.astype(jnp.bfloat16)
    loads[0].wait()
    docs = docs_buf[...]
    query_at = mine_q * rows + lax.broadcasted_iota(jnp.int32, (rows, 1), 0)
    query_at = query_at.astype(jnp.float32)
    begin = jnp.zeros((rows, 1), jnp.float32)
    for doc in range(3):
        cut = jnp.sum(jnp.where(docs <= doc, 1.0, 0.0), axis=0, keepdims=True)
        cut = jnp.sum(cut, axis=1, keepdims=True)
        begin = jnp.maximum(begin, jnp.where(cut <= query_at, cut, 0.0))

    loads[1].wait()
    cos_row, sin_row = table_buf[:rows], table_buf[rows : 2 * rows]
    lane = lax.broadcasted_iota(jnp.int32, (1, width), 1)
    sign = jnp.where(lane < width // 2, -1.0, 1.0)

    def row_of(slot):
        return slot * rows if isinstance(slot, int) else pl.multiple_of(slot * rows, rows)

    def angles(slot):
        first = jnp.maximum(mine_q - back + slot, 0)
        cos_block = table_buf[pl.ds(2 * rows + first, 1)]
        sin_block = table_buf[pl.ds(2 * rows + blocks + first, 1)]
        cosines[pl.ds(row_of(slot), rows)] = cos_row * cos_block - sin_row * sin_block
        sines[pl.ds(row_of(slot), rows)] = (sin_row * cos_block + cos_row * sin_block) * sign

    each(slots, angles)
    loads[2].wait()
    loads[3].wait()
    for g in range(kv):
        up_all[g, :rank, :width] = up_buf[0, g]
        up_all[g, rank:, width:] = up_buf[1, g]
    loads[4].wait()

    def hand_on(slot):
        return pltpu.make_async_remote_copy(
            src_ref=part_of(window.at[slot], core),
            dst_ref=part_of(window.at[slot], core),
            send_sem=pass_sem.at[slot],
            recv_sem=mate_sem.at[slot],
            device_id={"pb": pb, "ka": mate},
            device_id_type=MESH,
        )

    def mate_needs(slot):
        return (base + slot >= 0) & (slot >= 1 - core) & (slot <= 1 - core + back)

    def relay(slot):
        @pl.when(base + slot >= 0)
        def _():
            take_own(slot).wait()

        @pl.when(mate_needs(slot))
        def _():
            hand_on(slot).start()

    each(slots + 1, relay)

    def rebuild(slot):
        at = row_of(slot)
        where = core + slot

        @pl.when(base + where >= 0)
        def _():
            pltpu.make_async_copy(
                part_of(lat_hbm, 1 - core), part_of(window.at[where], 1 - core), mate_sem.at[where]
            ).wait()

        sorted_rows = jnp.dot(
            pick[...], window[where], preferred_element_type=jnp.float32
        ).astype(jnp.bfloat16)
        for g in range(kv):
            both = jnp.dot(
                sorted_rows[g * rows : (g + 1) * rows],
                up_all[g],
                preferred_element_type=jnp.float32,
            )
            key = both[:, :width]
            key = key * cosines[pl.ds(at, rows)]
            key = key + pltpu.roll(both[:, :width], width // 2, 1) * sines[pl.ds(at, rows)]
            keys[g, pl.ds(at, rows)] = key.astype(jnp.bfloat16)
            values[g, pl.ds(at, rows), :width] = both[:, width:].astype(jnp.bfloat16)

    each(slots, rebuild)

    factor = math.log2(math.e) * width ** (-0.5)
    reach = span * rows

    def attend(chunk):
        at = chunk * reach if isinstance(chunk, int) else pl.multiple_of(chunk * reach, reach)
        key_at = (mine_q - back + chunk * span) * rows
        key_at = key_at + lax.broadcasted_iota(jnp.int32, (1, reach), 1)
        key_at = key_at.astype(jnp.float32)
        bias = jnp.where((key_at >= begin) & (key_at <= query_at), 0.0, NEG)
        bias = jnp.concatenate([bias] * group, axis=0)
        for g in range(kv):
            heads = range(g * group, (g + 1) * group)
            stacked = jnp.concatenate([q_buf[:, h * width : (h + 1) * width] for h in heads])
            scores = lax.dot_general(
                stacked,
                keys[g, pl.ds(at, reach)],
                (((1,), (1,)), ((), ())),
                preferred_element_type=jnp.float32,
            )
            scores = scores + bias
            top = jnp.max(scores, axis=1, keepdims=True)
            if span < slots:
                before = row_max[g]
                top = jnp.maximum(top, before)
                row_max[g] = top
                scale = jnp.exp2((before - top) * factor)
            weights = jnp.exp2((scores - top) * factor).astype(jnp.bfloat16)
            part = jnp.dot(
                weights, values[g, pl.ds(at, reach)], preferred_element_type=jnp.float32
            )
            if span < slots:
                total[g] = total[g] * scale + part
            else:
                write(g, part)

    def write(g, part):
        ratio = (part[:, :width] / part[:, width:]).astype(jnp.bfloat16)
        for i in range(group):
            h = g * group + i
            out_ref[:, h * width : (h + 1) * width] = ratio[i * rows : (i + 1) * rows]

    if span < slots:
        row_max[...] = jnp.full(row_max.shape, NEG, jnp.float32)
        total[...] = jnp.zeros(total.shape, jnp.float32)
        lax.fori_loop(0, slots // span, lambda c, _: (attend(c), 0)[1], 0)
        for g in range(kv):
            write(g, total[g])
    else:
        attend(0)

    def drain(step):
        @pl.when(goes(step))
        def _():
            copy_to(step).wait_send()

    each(reached, drain)

    def drain_mate(slot):
        @pl.when(mate_needs(slot))
        def _():
            hand_on(slot).wait_send()

    each(slots + 1, drain_mate)


def shards(queries, latents, key_up, value_up, documents):
    rows = queries.shape[0]
    kv, rank, width = key_up.shape
    heads = queries.shape[1] // width
    npb, nka = lax.axis_size("pb"), lax.axis_size("ka")
    blocks = npb * nka
    tokens = documents.shape[0]
    back = -(-(tokens // 2 - 1) // rows)
    slots = back + 1
    span = max(d for d in range(1, 9) if slots % d == 0)
    many = span < slots
    table = jnp.asarray(rotary_tables(rows, blocks, width))
    plan = (rows, blocks, back, span, kv, heads // kv, width, rank, npb, nka)
    bf16, f32 = jnp.bfloat16, jnp.float32
    return pl.pallas_call(
        functools.partial(kernel, plan),
        out_shape=pltpu.VMEM(queries.shape, bf16),
        in_specs=[pl.BlockSpec(memory_space=pltpu.HBM)] * 6,
        out_specs=pl.BlockSpec(memory_space=pltpu.VMEM),
        scratch_shapes=[
            pltpu.VMEM(queries.shape, bf16),
            pltpu.VMEM((2, kv, rank, width), bf16),
            pltpu.VMEM((tokens // 128, 128), jnp.int32),
            pltpu.VMEM(table.shape, f32),
            pltpu.VMEM((rows * kv, rows * kv), bf16),
            pltpu.VMEM((slots * rows, width), f32),
            pltpu.VMEM((slots * rows, width), f32),
            pltpu.VMEM((slots + 1, rows * kv, 2 * rank), bf16),
            pltpu.VMEM((kv, 2 * rank, 2 * width), bf16),
            pltpu.VMEM((kv, slots * rows, width), bf16),
            pltpu.VMEM((kv, slots * rows, 2 * width), bf16),
            pltpu.VMEM((kv, heads // kv * rows if many else 8, 1), f32),
            pltpu.VMEM((kv, heads // kv * rows if many else 8, 2 * width), f32),
            pltpu.SemaphoreType.DMA((5,)),
            pltpu.SemaphoreType.DMA((slots + 2,)),
            pltpu.SemaphoreType.DMA((slots + 1,)),
            pltpu.SemaphoreType.DMA((slots + 1,)),
            pltpu.SemaphoreType.DMA((slots + 1,)),
        ],
        compiler_params=pltpu.CompilerParams(
            collective_id=0, has_side_effects=True, vmem_limit_bytes=63 * 2**20
        ),
    )(
        queries,
        latents.reshape(rows * kv, 2 * rank),
        key_up,
        value_up,
        documents.reshape(tokens // 128, 128),
        table,
    )


def solution(mesh):
    placed = (
        P(("pb", "ka"), "ha"),
        P(("ka", "pb"), "ha", None),
        P("ha", None, None),
        P("ha", None, None),
        P(),
    )
    return jax.shard_map(
        shards, mesh=mesh, in_specs=placed, out_specs=P(("pb", "ka"), "ha"), check_vma=False
    )
```

```python
import functools
import math

import jax
import jax.numpy as jnp
import numpy as np
from jax import lax
from jax.experimental import pallas as pl
from jax.experimental.pallas import tpu as pltpu
from jax.sharding import PartitionSpec as P

NEG = -1e30
MESH = pl.DeviceIdType.MESH


def rotary_tables(rows, blocks, width):
    half = np.arange(width // 2, dtype=np.float64)
    base = 500000.0 ** (-2.0 * half / width)
    wave = 2.0 * np.pi / base
    smooth = (8192.0 / wave - 1.0) / 3.0
    blended = (1.0 - smooth) * base / 8.0 + smooth * base
    freq = np.where(wave < 2048.0, base, np.where(wave > 8192.0, base / 8.0, blended))
    freq = np.concatenate([freq, freq])
    inner = np.arange(rows)[:, None] * freq
    outer = (np.arange(blocks) * rows)[:, None] * freq
    return np.concatenate(
        [np.cos(inner), np.sin(inner), np.cos(outer), np.sin(outer)], axis=0
    ).astype(np.float32)


def split(number, size):
    if size & (size - 1):
        return lax.div(number, size), lax.rem(number, size)
    return lax.shift_right_logical(number, size.bit_length() - 1), number & (size - 1)


def each(count, body):
    if count <= 8:
        for index in range(count):
            body(index)
    else:
        lax.fori_loop(0, count, lambda index, _: (body(index), 0)[1], 0)


def kernel(
    plan,
    q_hbm,
    lat_hbm,
    key_up_hbm,
    value_up_hbm,
    docs_hbm,
    table_hbm,
    out_ref,
    q_buf,
    lat_buf,
    up_buf,
    docs_buf,
    table_buf,
    stage,
    window,
    cosines,
    sines,
    up_all,
    keys,
    values,
    row_max,
    total,
    in_sem,
    send_sem,
    recv_sem,
):
    rows, blocks, back, span, kv, group, width, rank, npb, nka = plan
    slots = back + 1
    pb, ka = lax.axis_index("pb"), lax.axis_index("ka")
    mine_q = pb * nka + ka
    mine_l = ka * npb + pb
    barrier = pltpu.get_barrier_semaphore()

    def greet(slot):
        source = mine_q - back + slot

        @pl.when((source >= 0) & (source != mine_l))
        def _():
            at_ka, at_pb = split(source, npb)
            pl.semaphore_signal(
                barrier, inc=1, device_id={"pb": at_pb, "ka": at_ka}, device_id_type=MESH
            )

    each(slots, greet)

    loads = [
        pltpu.make_async_copy(lat_hbm, lat_buf, in_sem.at[0]),
        pltpu.make_async_copy(key_up_hbm, up_buf.at[0], in_sem.at[1]),
        pltpu.make_async_copy(value_up_hbm, up_buf.at[1], in_sem.at[2]),
        pltpu.make_async_copy(docs_hbm, docs_buf, in_sem.at[3]),
        pltpu.make_async_copy(table_hbm, table_buf, in_sem.at[4]),
        pltpu.make_async_copy(q_hbm, q_buf, in_sem.at[5]),
    ]
    for load in loads:
        load.start()

    def clear(slot):
        @pl.when(mine_q - back + slot < 0)
        def _():
            window[slot] = jnp.zeros(window.shape[1:], window.dtype)

    each(slots, clear)

    loads[0].wait()
    place = lax.broadcasted_iota(jnp.int32, (kv * rows, kv * rows), 0)
    col = lax.broadcasted_iota(jnp.int32, (kv * rows, kv * rows), 1)
    pick = jnp.zeros((kv * rows, kv * rows), jnp.float32)
    for g in range(kv):
        here = (place >= g * rows) & (place < (g + 1) * rows)
        pick = jnp.where(here & (col == (place - g * rows) * kv + g), 1.0, pick)
    stage[...] = jnp.dot(
        pick.astype(jnp.bfloat16), lat_buf[...], preferred_element_type=jnp.float32
    ).astype(jnp.bfloat16)

    last = jnp.minimum(blocks - 1, mine_l + back)
    own = ((mine_q >= mine_l) & (mine_q <= last)).astype(jnp.int32)
    partners = last - mine_l + 1 - own

    @pl.when(partners > 0)
    def _():
        pl.semaphore_wait(barrier, partners)

    def copy_to(step):
        at_pb, at_ka = split(mine_l + step, nka)
        return pltpu.make_async_remote_copy(
            src_ref=stage,
            dst_ref=window.at[back - step],
            send_sem=send_sem.at[step],
            recv_sem=recv_sem.at[back - step],
            device_id={"pb": at_pb, "ka": at_ka},
            device_id_type=MESH,
        )

    def send(step):
        target = mine_l + step

        @pl.when((target < blocks) & (target != mine_q))
        def _():
            copy_to(step).start()

        @pl.when(target == mine_q)
        def _():
            window[back - step] = stage[...]

    each(slots, send)

    loads[1].wait()
    loads[2].wait()
    up_all[...] = jnp.zeros(up_all.shape, up_all.dtype)
    for g in range(kv):
        up_all[g, :rank, :width] = up_buf[0, g]
        up_all[g, rank:, width:] = up_buf[1, g]
    loads[3].wait()
    docs = docs_buf[...]
    query_at = mine_q * rows + lax.broadcasted_iota(jnp.int32, (rows, 1), 0)
    query_at = query_at.astype(jnp.float32)
    begin = jnp.zeros((rows, 1), jnp.float32)
    for doc in range(3):
        cut = jnp.sum(jnp.where(docs <= doc, 1.0, 0.0), axis=0, keepdims=True)
        cut = jnp.sum(cut, axis=1, keepdims=True)
        begin = jnp.maximum(begin, jnp.where(cut <= query_at, cut, 0.0))

    loads[4].wait()
    cos_row, sin_row = table_buf[:rows], table_buf[rows : 2 * rows]
    lane = lax.broadcasted_iota(jnp.int32, (1, width), 1)
    sign = jnp.where(lane < width // 2, -1.0, 1.0)

    def row_of(slot):
        return slot * rows if isinstance(slot, int) else pl.multiple_of(slot * rows, rows)

    def angles(slot):
        first = jnp.maximum(mine_q - back + slot, 0)
        cos_block = table_buf[pl.ds(2 * rows + first, 1)]
        sin_block = table_buf[pl.ds(2 * rows + blocks + first, 1)]
        cosines[pl.ds(row_of(slot), rows)] = cos_row * cos_block - sin_row * sin_block
        sines[pl.ds(row_of(slot), rows)] = (sin_row * cos_block + cos_row * sin_block) * sign

    each(slots, angles)
    values[:, :, width:] = jnp.ones((kv, slots * rows, width), jnp.bfloat16)

    def bias_of(first, count):
        key_at = (mine_q - back + first) * rows
        key_at = key_at + lax.broadcasted_iota(jnp.int32, (1, count * rows), 1)
        key_at = key_at.astype(jnp.float32)
        return jnp.where((key_at >= begin) & (key_at <= query_at), 0.0, NEG)

    def arrive(slot):
        source = mine_q - back + slot

        @pl.when((source >= 0) & (source != mine_l))
        def _():
            pltpu.make_async_copy(stage, window.at[slot], recv_sem.at[slot]).wait()

    def rebuild(first, count):
        at, reach = row_of(first), count * rows
        for g in range(kv):
            latents = [window[first + i, g * rows : (g + 1) * rows] for i in range(count)]
            both = jnp.dot(
                jnp.concatenate(latents), up_all[g], preferred_element_type=jnp.float32
            )
            key = both[:, :width] * cosines[pl.ds(at, reach)]
            key = key + pltpu.roll(both[:, :width], width // 2, 1) * sines[pl.ds(at, reach)]
            keys[g, pl.ds(at, reach)] = key.astype(jnp.bfloat16)
            values[g, pl.ds(at, reach), :width] = both[:, width:].astype(jnp.bfloat16)

    factor = math.log2(math.e) * width ** (-0.5)

    def attend(g, first, count, bias, before, sums):
        at, reach = row_of(first), count * rows
        heads = range(g * group, (g + 1) * group)
        stacked = jnp.concatenate([q_buf[:, h * width : (h + 1) * width] for h in heads])
        scores = lax.dot_general(
            stacked,
            keys[g, pl.ds(at, reach)],
            (((1,), (1,)), ((), ())),
            preferred_element_type=jnp.float32,
        )
        scores = scores + jnp.concatenate([bias] * group)
        top = jnp.max(scores, axis=1, keepdims=True)
        if before is not None:
            top = jnp.maximum(top, before)
        weights = jnp.exp2((scores - top) * factor).astype(jnp.bfloat16)
        part = jnp.dot(weights, values[g, pl.ds(at, reach)], preferred_element_type=jnp.float32)
        if before is not None:
            part = part + sums * jnp.exp2((before - top) * factor)
        return top, part

    def write(g, part):
        ratio = (part[:, :width] / part[:, width:]).astype(jnp.bfloat16)
        for i in range(group):
            h = g * group + i
            out_ref[:, h * width : (h + 1) * width] = ratio[i * rows : (i + 1) * rows]

    def drain(step):
        target = mine_l + step

        @pl.when((target < blocks) & (target != mine_q))
        def _():
            copy_to(step).wait_send()

    if slots <= 8:
        mask = bias_of(0, slots)
        loads[5].wait()
        for slot in reversed(range(slots)):
            arrive(slot)
            if slot == 1:
                each(slots, drain)
        rebuild(0, slots)
        for g in range(kv):
            write(g, attend(g, 0, slots, mask, None, None)[1])
    else:
        row_max[...] = jnp.full(row_max.shape, NEG, jnp.float32)
        total[...] = jnp.zeros(total.shape, jnp.float32)
        loads[5].wait()

        def run(chunk, _):
            for i in range(span):
                arrive(chunk * span + i)
            rebuild(chunk * span, span)
            mask = bias_of(chunk * span, span)
            for g in range(kv):
                row_max[g], total[g] = attend(
                    g, chunk * span, span, mask, row_max[g], total[g]
                )
            return 0

        lax.fori_loop(0, slots // span, run, 0)
        for g in range(kv):
            write(g, total[g])
        each(slots, drain)


def shards(queries, latents, key_up, value_up, documents):
    rows = queries.shape[0]
    kv, rank, width = key_up.shape
    heads = queries.shape[1] // width
    npb, nka = lax.axis_size("pb"), lax.axis_size("ka")
    blocks = npb * nka
    tokens = documents.shape[0]
    back = -(-(tokens // 2 - 1) // rows)
    slots = back + 1
    span = max(d for d in range(1, 9) if slots % d == 0)
    many = slots > 8
    table = jnp.asarray(rotary_tables(rows, blocks, width))
    plan = (rows, blocks, back, span, kv, heads // kv, width, rank, npb, nka)
    bf16, f32 = jnp.bfloat16, jnp.float32
    return pl.pallas_call(
        functools.partial(kernel, plan),
        out_shape=pltpu.VMEM(queries.shape, bf16),
        in_specs=[pl.BlockSpec(memory_space=pltpu.HBM)] * 6,
        out_specs=pl.BlockSpec(memory_space=pltpu.VMEM),
        scratch_shapes=[
            pltpu.VMEM(queries.shape, bf16),
            pltpu.VMEM((rows * kv, 2 * rank), bf16),
            pltpu.VMEM((2, kv, rank, width), bf16),
            pltpu.VMEM((tokens // 128, 128), jnp.int32),
            pltpu.VMEM(table.shape, f32),
            pltpu.VMEM((rows * kv, 2 * rank), bf16),
            pltpu.VMEM((slots, rows * kv, 2 * rank), bf16),
            pltpu.VMEM((slots * rows, width), f32),
            pltpu.VMEM((slots * rows, width), f32),
            pltpu.VMEM((kv, 2 * rank, 2 * width), bf16),
            pltpu.VMEM((kv, slots * rows, width), bf16),
            pltpu.VMEM((kv, slots * rows, 2 * width), bf16),
            pltpu.VMEM((kv, heads // kv * rows if many else 8, 1), f32),
            pltpu.VMEM((kv, heads // kv * rows if many else 8, 2 * width), f32),
            pltpu.SemaphoreType.DMA((6,)),
            pltpu.SemaphoreType.DMA((slots,)),
            pltpu.SemaphoreType.DMA((slots,)),
        ],
        compiler_params=pltpu.CompilerParams(
            collective_id=0, has_side_effects=True, vmem_limit_bytes=63 * 2**20
        ),
    )(
        queries,
        latents.reshape(rows * kv, 2 * rank),
        key_up,
        value_up,
        documents.reshape(tokens // 128, 128),
        table,
    )


def solution(mesh):
    placed = (
        P(("pb", "ka"), "ha"),
        P(("ka", "pb"), "ha", None),
        P("ha", None, None),
        P("ha", None, None),
        P(),
    )
    return jax.shard_map(
        shards, mesh=mesh, in_specs=placed, out_specs=P(("pb", "ka"), "ha"), check_vma=False
    )
```

```python
import functools
import math

import jax
import jax.numpy as jnp
import numpy as np
from jax import lax
from jax.experimental import pallas as pl
from jax.experimental.pallas import tpu as pltpu
from jax.sharding import PartitionSpec as P

NEG = -1e30
MESH = pl.DeviceIdType.MESH


def rotary_tables(rows, blocks, width):
    half = np.arange(width // 2, dtype=np.float64)
    base = 500000.0 ** (-2.0 * half / width)
    wave = 2.0 * np.pi / base
    smooth = (8192.0 / wave - 1.0) / 3.0
    blended = (1.0 - smooth) * base / 8.0 + smooth * base
    freq = np.where(wave < 2048.0, base, np.where(wave > 8192.0, base / 8.0, blended))
    freq = np.concatenate([freq, freq])
    inner = np.arange(rows)[:, None] * freq
    outer = (np.arange(blocks) * rows)[:, None] * freq
    return np.concatenate(
        [np.cos(inner), np.sin(inner), np.cos(outer), np.sin(outer)], axis=0
    ).astype(np.float32)


def split(number, size):
    if size & (size - 1):
        return lax.div(number, size), lax.rem(number, size)
    return lax.shift_right_logical(number, size.bit_length() - 1), number & (size - 1)


def each(count, body):
    if count <= 8:
        for index in range(count):
            body(index)
    else:
        lax.fori_loop(0, count, lambda index, _: (body(index), 0)[1], 0)


def kernel(
    plan,
    q_hbm,
    lat_hbm,
    key_up_hbm,
    value_up_hbm,
    docs_hbm,
    table_hbm,
    out_ref,
    q_buf,
    lat_buf,
    up_buf,
    docs_buf,
    table_buf,
    stage,
    window,
    cosines,
    sines,
    up_all,
    keys,
    values,
    row_max,
    total,
    in_sem,
    send_sem,
    recv_sem,
):
    rows, blocks, back, span, kv, group, width, rank, npb, nka = plan
    slots = back + 1
    pb, ka = lax.axis_index("pb"), lax.axis_index("ka")
    mine_q = pb * nka + ka
    mine_l = ka * npb + pb
    barrier = pltpu.get_barrier_semaphore()

    def greet(slot):
        source = mine_q - back + slot

        @pl.when((source >= 0) & (source != mine_l))
        def _():
            at_ka, at_pb = split(source, npb)
            pl.semaphore_signal(
                barrier, inc=1, device_id={"pb": at_pb, "ka": at_ka}, device_id_type=MESH
            )

    each(slots, greet)

    loads = [
        pltpu.make_async_copy(lat_hbm, lat_buf, in_sem.at[0]),
        pltpu.make_async_copy(key_up_hbm, up_buf.at[0], in_sem.at[1]),
        pltpu.make_async_copy(value_up_hbm, up_buf.at[1], in_sem.at[2]),
        pltpu.make_async_copy(docs_hbm, docs_buf, in_sem.at[3]),
        pltpu.make_async_copy(table_hbm, table_buf, in_sem.at[4]),
        pltpu.make_async_copy(q_hbm, q_buf, in_sem.at[5]),
    ]
    for load in loads:
        load.start()

    def clear(slot):
        @pl.when(mine_q - back + slot < 0)
        def _():
            window[slot] = jnp.zeros(window.shape[1:], window.dtype)

    each(slots, clear)

    loads[0].wait()
    place = lax.broadcasted_iota(jnp.int32, (kv * rows, kv * rows), 0)
    col = lax.broadcasted_iota(jnp.int32, (kv * rows, kv * rows), 1)
    pick = jnp.zeros((kv * rows, kv * rows), jnp.float32)
    for g in range(kv):
        here = (place >= g * rows) & (place < (g + 1) * rows)
        pick = jnp.where(here & (col == (place - g * rows) * kv + g), 1.0, pick)
    stage[...] = jnp.dot(
        pick.astype(jnp.bfloat16), lat_buf[...], preferred_element_type=jnp.float32
    ).astype(jnp.bfloat16)

    def keep(step):
        @pl.when(mine_l + step == mine_q)
        def _():
            window[back - step] = stage[...]

    each(slots, keep)

    last = jnp.minimum(blocks - 1, mine_l + back)
    own = ((mine_q >= mine_l) & (mine_q <= last)).astype(jnp.int32)
    partners = last - mine_l + 1 - own

    @pl.when(partners > 0)
    def _():
        pl.semaphore_wait(barrier, partners)

    def copy_to(step):
        at_pb, at_ka = split(mine_l + step, nka)
        return pltpu.make_async_remote_copy(
            src_ref=stage,
            dst_ref=window.at[back - step],
            send_sem=send_sem.at[step],
            recv_sem=recv_sem.at[back - step],
            device_id={"pb": at_pb, "ka": at_ka},
            device_id_type=MESH,
        )

    def send(step):
        target = mine_l + step

        @pl.when((target < blocks) & (target != mine_q))
        def _():
            copy_to(step).start()

    each(slots, send)

    loads[1].wait()
    loads[2].wait()
    up_all[...] = jnp.zeros(up_all.shape, up_all.dtype)
    for g in range(kv):
        up_all[g, :rank, :width] = up_buf[0, g]
        up_all[g, rank:, width:] = up_buf[1, g]
    loads[3].wait()
    docs = docs_buf[...]
    query_at = mine_q * rows + lax.broadcasted_iota(jnp.int32, (rows, 1), 0)
    query_at = query_at.astype(jnp.float32)
    begin = jnp.zeros((rows, 1), jnp.float32)
    for doc in range(3):
        cut = jnp.sum(jnp.where(docs <= doc, 1.0, 0.0), axis=0, keepdims=True)
        cut = jnp.sum(cut, axis=1, keepdims=True)
        begin = jnp.maximum(begin, jnp.where(cut <= query_at, cut, 0.0))

    loads[4].wait()
    cos_row, sin_row = table_buf[:rows], table_buf[rows : 2 * rows]
    lane = lax.broadcasted_iota(jnp.int32, (1, width), 1)
    sign = jnp.where(lane < width // 2, -1.0, 1.0)

    def row_of(slot):
        return slot * rows if isinstance(slot, int) else pl.multiple_of(slot * rows, rows)

    def angles(slot):
        first = jnp.maximum(mine_q - back + slot, 0)
        cos_block = table_buf[pl.ds(2 * rows + first, 1)]
        sin_block = table_buf[pl.ds(2 * rows + blocks + first, 1)]
        cosines[pl.ds(row_of(slot), rows)] = cos_row * cos_block - sin_row * sin_block
        sines[pl.ds(row_of(slot), rows)] = (sin_row * cos_block + cos_row * sin_block) * sign

    each(slots, angles)
    values[:, :, width:] = jnp.ones((kv, slots * rows, width), jnp.bfloat16)

    def bias_of(first, count):
        key_at = (mine_q - back + first) * rows
        key_at = key_at + lax.broadcasted_iota(jnp.int32, (1, count * rows), 1)
        key_at = key_at.astype(jnp.float32)
        return jnp.where((key_at >= begin) & (key_at <= query_at), 0.0, NEG)

    def arrive(slot):
        source = mine_q - back + slot

        @pl.when((source >= 0) & (source != mine_l))
        def _():
            pltpu.make_async_copy(stage, window.at[slot], recv_sem.at[slot]).wait()

    def rebuild(first, count):
        at, reach = row_of(first), count * rows
        for g in range(kv):
            latents = [window[first + i, g * rows : (g + 1) * rows] for i in range(count)]
            both = jnp.dot(
                jnp.concatenate(latents), up_all[g], preferred_element_type=jnp.float32
            )
            key = both[:, :width] * cosines[pl.ds(at, reach)]
            key = key + pltpu.roll(both[:, :width], width // 2, 1) * sines[pl.ds(at, reach)]
            keys[g, pl.ds(at, reach)] = key.astype(jnp.bfloat16)
            values[g, pl.ds(at, reach), :width] = both[:, width:].astype(jnp.bfloat16)

    factor = math.log2(math.e) * width ** (-0.5)

    def attend(g, first, count, bias, before, sums):
        at, reach = row_of(first), count * rows
        heads = range(g * group, (g + 1) * group)
        stacked = jnp.concatenate([q_buf[:, h * width : (h + 1) * width] for h in heads])
        scores = lax.dot_general(
            stacked,
            keys[g, pl.ds(at, reach)],
            (((1,), (1,)), ((), ())),
            preferred_element_type=jnp.float32,
        )
        scores = scores + jnp.concatenate([bias] * group)
        top = jnp.max(scores, axis=1, keepdims=True)
        if before is not None:
            top = jnp.maximum(top, before)
        weights = jnp.exp2((scores - top) * factor).astype(jnp.bfloat16)
        part = jnp.dot(weights, values[g, pl.ds(at, reach)], preferred_element_type=jnp.float32)
        if before is not None:
            part = part + sums * jnp.exp2((before - top) * factor)
        return top, part

    def write(g, part):
        ratio = (part[:, :width] / part[:, width:]).astype(jnp.bfloat16)
        for i in range(group):
            h = g * group + i
            out_ref[:, h * width : (h + 1) * width] = ratio[i * rows : (i + 1) * rows]

    def drain(step):
        target = mine_l + step

        @pl.when((target < blocks) & (target != mine_q))
        def _():
            copy_to(step).wait_send()

    if slots <= 8:
        mask = bias_of(0, slots)
        loads[5].wait()
        for slot in reversed(range(slots)):
            arrive(slot)
        rebuild(0, slots)
        for g in range(kv):
            write(g, attend(g, 0, slots, mask, None, None)[1])
        each(slots, drain)
    else:
        row_max[...] = jnp.full(row_max.shape, NEG, jnp.float32)
        total[...] = jnp.zeros(total.shape, jnp.float32)
        loads[5].wait()

        def run(chunk, _):
            for i in range(span):
                arrive(chunk * span + i)
            rebuild(chunk * span, span)
            mask = bias_of(chunk * span, span)
            for g in range(kv):
                row_max[g], total[g] = attend(
                    g, chunk * span, span, mask, row_max[g], total[g]
                )
            return 0

        lax.fori_loop(0, slots // span, run, 0)
        for g in range(kv):
            write(g, total[g])
        each(slots, drain)


def shards(queries, latents, key_up, value_up, documents):
    rows = queries.shape[0]
    kv, rank, width = key_up.shape
    heads = queries.shape[1] // width
    npb, nka = lax.axis_size("pb"), lax.axis_size("ka")
    blocks = npb * nka
    tokens = documents.shape[0]
    back = -(-(tokens // 2 - 1) // rows)
    slots = back + 1
    span = max(d for d in range(1, 9) if slots % d == 0)
    many = slots > 8
    table = jnp.asarray(rotary_tables(rows, blocks, width))
    plan = (rows, blocks, back, span, kv, heads // kv, width, rank, npb, nka)
    bf16, f32 = jnp.bfloat16, jnp.float32
    return pl.pallas_call(
        functools.partial(kernel, plan),
        out_shape=pltpu.VMEM(queries.shape, bf16),
        in_specs=[pl.BlockSpec(memory_space=pltpu.HBM)] * 6,
        out_specs=pl.BlockSpec(memory_space=pltpu.VMEM),
        scratch_shapes=[
            pltpu.VMEM(queries.shape, bf16),
            pltpu.VMEM((rows * kv, 2 * rank), bf16),
            pltpu.VMEM((2, kv, rank, width), bf16),
            pltpu.VMEM((tokens // 128, 128), jnp.int32),
            pltpu.VMEM(table.shape, f32),
            pltpu.VMEM((rows * kv, 2 * rank), bf16),
            pltpu.VMEM((slots, rows * kv, 2 * rank), bf16),
            pltpu.VMEM((slots * rows, width), f32),
            pltpu.VMEM((slots * rows, width), f32),
            pltpu.VMEM((kv, 2 * rank, 2 * width), bf16),
            pltpu.VMEM((kv, slots * rows, width), bf16),
            pltpu.VMEM((kv, slots * rows, 2 * width), bf16),
            pltpu.VMEM((kv, heads // kv * rows if many else 8, 1), f32),
            pltpu.VMEM((kv, heads // kv * rows if many else 8, 2 * width), f32),
            pltpu.SemaphoreType.DMA((6,)),
            pltpu.SemaphoreType.DMA((slots,)),
            pltpu.SemaphoreType.DMA((slots,)),
        ],
        compiler_params=pltpu.CompilerParams(
            collective_id=0, has_side_effects=True, vmem_limit_bytes=63 * 2**20
        ),
    )(
        queries,
        latents.reshape(rows * kv, 2 * rank),
        key_up,
        value_up,
        documents.reshape(tokens // 128, 128),
        table,
    )


def solution(mesh):
    placed = (
        P(("pb", "ka"), "ha"),
        P(("ka", "pb"), "ha", None),
        P("ha", None, None),
        P("ha", None, None),
        P(),
    )
    return jax.shard_map(
        shards, mesh=mesh, in_specs=placed, out_specs=P(("pb", "ka"), "ha"), check_vma=False
    )
```

```python
import functools
import math

import jax
import jax.numpy as jnp
import numpy as np
from jax import lax
from jax.experimental import pallas as pl
from jax.experimental.pallas import tpu as pltpu
from jax.sharding import PartitionSpec as P

NEG = -1e30
MESH = pl.DeviceIdType.MESH


def rotary_tables(rows, blocks, width):
    half = np.arange(width // 2, dtype=np.float64)
    base = 500000.0 ** (-2.0 * half / width)
    wave = 2.0 * np.pi / base
    smooth = (8192.0 / wave - 1.0) / 3.0
    blended = (1.0 - smooth) * base / 8.0 + smooth * base
    freq = np.where(wave < 2048.0, base, np.where(wave > 8192.0, base / 8.0, blended))
    freq = np.concatenate([freq, freq])
    inner = np.arange(rows)[:, None] * freq
    outer = (np.arange(blocks) * rows)[:, None] * freq
    return np.concatenate(
        [np.cos(inner), np.sin(inner), np.cos(outer), np.sin(outer)], axis=0
    ).astype(np.float32)


def split(number, size):
    if size & (size - 1):
        return lax.div(number, size), lax.rem(number, size)
    return lax.shift_right_logical(number, size.bit_length() - 1), number & (size - 1)


def each(count, body):
    if count <= 8:
        for index in range(count):
            body(index)
    else:
        lax.fori_loop(0, count, lambda index, _: (body(index), 0)[1], 0)


def kernel(
    plan,
    q_hbm,
    lat_hbm,
    key_up_hbm,
    value_up_hbm,
    docs_hbm,
    table_hbm,
    out_ref,
    q_buf,
    lat_buf,
    up_buf,
    docs_buf,
    table_buf,
    stage,
    window,
    cosines,
    sines,
    up_all,
    keys,
    values,
    row_max,
    total,
    in_sem,
    send_sem,
    recv_sem,
):
    rows, blocks, back, span, kv, group, width, rank, npb, nka = plan
    slots = back + 1
    pb, ka = lax.axis_index("pb"), lax.axis_index("ka")
    mine_q = pb * nka + ka
    mine_l = ka * npb + pb
    barrier = pltpu.get_barrier_semaphore()

    def greet(slot):
        source = mine_q - back + slot

        @pl.when((source >= 0) & (source != mine_l))
        def _():
            at_ka, at_pb = split(source, npb)
            pl.semaphore_signal(
                barrier, inc=1, device_id={"pb": at_pb, "ka": at_ka}, device_id_type=MESH
            )

    each(slots, greet)

    loads = [
        pltpu.make_async_copy(lat_hbm, lat_buf, in_sem.at[0]),
        pltpu.make_async_copy(key_up_hbm, up_buf.at[0], in_sem.at[1]),
        pltpu.make_async_copy(value_up_hbm, up_buf.at[1], in_sem.at[2]),
        pltpu.make_async_copy(docs_hbm, docs_buf, in_sem.at[3]),
        pltpu.make_async_copy(table_hbm, table_buf, in_sem.at[4]),
        pltpu.make_async_copy(q_hbm, q_buf, in_sem.at[5]),
    ]
    for load in loads:
        load.start()

    def clear(slot):
        @pl.when(mine_q - back + slot < 0)
        def _():
            window[slot] = jnp.zeros(window.shape[1:], window.dtype)

    each(slots, clear)

    loads[0].wait()
    place = lax.broadcasted_iota(jnp.int32, (kv * rows, kv * rows), 0)
    col = lax.broadcasted_iota(jnp.int32, (kv * rows, kv * rows), 1)
    pick = jnp.zeros((kv * rows, kv * rows), jnp.float32)
    for g in range(kv):
        here = (place >= g * rows) & (place < (g + 1) * rows)
        pick = jnp.where(here & (col == (place - g * rows) * kv + g), 1.0, pick)
    stage[...] = jnp.dot(
        pick.astype(jnp.bfloat16), lat_buf[...], preferred_element_type=jnp.float32
    ).astype(jnp.bfloat16)

    def keep(step):
        @pl.when(mine_l + step == mine_q)
        def _():
            window[back - step] = stage[...]

    each(slots, keep)

    last = jnp.minimum(blocks - 1, mine_l + back)
    own = ((mine_q >= mine_l) & (mine_q <= last)).astype(jnp.int32)
    partners = last - mine_l + 1 - own

    @pl.when(partners > 0)
    def _():
        pl.semaphore_wait(barrier, partners)

    def copy_to(step):
        at_pb, at_ka = split(mine_l + step, nka)
        return pltpu.make_async_remote_copy(
            src_ref=stage,
            dst_ref=window.at[back - step],
            send_sem=send_sem.at[step],
            recv_sem=recv_sem.at[back - step],
            device_id={"pb": at_pb, "ka": at_ka},
            device_id_type=MESH,
        )

    def send(step):
        target = mine_l + step

        @pl.when((target < blocks) & (target != mine_q))
        def _():
            copy_to(step).start()

    each(slots, send)

    loads[1].wait()
    loads[2].wait()
    up_all[...] = jnp.zeros(up_all.shape, up_all.dtype)
    for g in range(kv):
        up_all[g, :rank, :width] = up_buf[0, g]
        up_all[g, rank:, width:] = up_buf[1, g]
    loads[3].wait()
    docs = docs_buf[...]
    query_at = mine_q * rows + lax.broadcasted_iota(jnp.int32, (rows, 1), 0)
    query_at = query_at.astype(jnp.float32)
    begin = jnp.zeros((rows, 1), jnp.float32)
    for doc in range(3):
        cut = jnp.sum(jnp.where(docs <= doc, 1.0, 0.0), axis=0, keepdims=True)
        cut = jnp.sum(cut, axis=1, keepdims=True)
        begin = jnp.maximum(begin, jnp.where(cut <= query_at, cut, 0.0))

    loads[4].wait()
    cos_row, sin_row = table_buf[:rows], table_buf[rows : 2 * rows]
    lane = lax.broadcasted_iota(jnp.int32, (1, width), 1)
    sign = jnp.where(lane < width // 2, -1.0, 1.0)

    def row_of(slot):
        return slot * rows if isinstance(slot, int) else pl.multiple_of(slot * rows, rows)

    def angles(slot):
        first = jnp.maximum(mine_q - back + slot, 0)
        cos_block = table_buf[pl.ds(2 * rows + first, 1)]
        sin_block = table_buf[pl.ds(2 * rows + blocks + first, 1)]
        cosines[pl.ds(row_of(slot), rows)] = cos_row * cos_block - sin_row * sin_block
        sines[pl.ds(row_of(slot), rows)] = (sin_row * cos_block + cos_row * sin_block) * sign

    each(slots, angles)
    values[:, :, width:] = jnp.ones((kv, slots * rows, width), jnp.bfloat16)

    def bias_of(first, count):
        key_at = (mine_q - back + first) * rows
        key_at = key_at + lax.broadcasted_iota(jnp.int32, (1, count * rows), 1)
        key_at = key_at.astype(jnp.float32)
        return jnp.where((key_at >= begin) & (key_at <= query_at), 0.0, NEG)

    def arrive(slot):
        source = mine_q - back + slot

        @pl.when((source >= 0) & (source != mine_l))
        def _():
            pltpu.make_async_copy(stage, window.at[slot], recv_sem.at[slot]).wait()

    def rebuild(first, count):
        at, reach = row_of(first), count * rows
        for g in range(kv):
            latents = [window[first + i, g * rows : (g + 1) * rows] for i in range(count)]
            both = jnp.dot(
                jnp.concatenate(latents), up_all[g], preferred_element_type=jnp.float32
            )
            key = both[:, :width] * cosines[pl.ds(at, reach)]
            key = key + pltpu.roll(both[:, :width], width // 2, 1) * sines[pl.ds(at, reach)]
            keys[g, pl.ds(at, reach)] = key.astype(jnp.bfloat16)
            values[g, pl.ds(at, reach), :width] = both[:, width:].astype(jnp.bfloat16)

    factor = math.log2(math.e) * width ** (-0.5)

    def attend(g, first, count, bias, before, sums):
        at, reach = row_of(first), count * rows
        heads = range(g * group, (g + 1) * group)
        stacked = jnp.concatenate([q_buf[:, h * width : (h + 1) * width] for h in heads])
        scores = lax.dot_general(
            stacked,
            keys[g, pl.ds(at, reach)],
            (((1,), (1,)), ((), ())),
            preferred_element_type=jnp.float32,
        )
        scores = scores + jnp.concatenate([bias] * group)
        top = jnp.max(scores, axis=1, keepdims=True)
        if before is not None:
            top = jnp.maximum(top, before)
        weights = jnp.exp2((scores - top) * factor).astype(jnp.bfloat16)
        part = jnp.dot(weights, values[g, pl.ds(at, reach)], preferred_element_type=jnp.float32)
        if before is not None:
            part = part + sums * jnp.exp2((before - top) * factor)
        return top, part

    def attend_t(g):
        heads = range(g * group, (g + 1) * group)
        stacked = jnp.concatenate([q_buf[:, h * width : (h + 1) * width] for h in heads])
        scores = lax.dot_general(
            keys[g], stacked, (((1,), (1,)), ((), ())), preferred_element_type=jnp.float32
        )
        scores = scores + mask_t
        top = jnp.max(scores, axis=0, keepdims=True)
        weights = jnp.exp2((scores - top) * factor).astype(jnp.bfloat16)
        return lax.dot_general(
            weights, values[g], (((0,), (0,)), ((), ())), preferred_element_type=jnp.float32
        )

    def write(g, part):
        ratio = (part[:, :width] / part[:, width:]).astype(jnp.bfloat16)
        for i in range(group):
            h = g * group + i
            out_ref[:, h * width : (h + 1) * width] = ratio[i * rows : (i + 1) * rows]

    def drain(step):
        target = mine_l + step

        @pl.when((target < blocks) & (target != mine_q))
        def _():
            copy_to(step).wait_send()

    if slots <= 8:
        key_col = (mine_q - back) * rows + lax.broadcasted_iota(jnp.int32, (slots * rows, 1), 0)
        key_col = key_col.astype(jnp.float32)
        q_lane = lax.broadcasted_iota(jnp.int32, (1, group * rows), 1)
        turn = q_lane
        for i in range(1, group):
            turn = jnp.where(q_lane >= i * rows, q_lane - i * rows, turn)
        turn = (mine_q * rows + turn).astype(jnp.float32)
        begin_t = jnp.zeros((1, group * rows), jnp.float32)
        for doc in range(3):
            cut = jnp.sum(jnp.where(docs <= doc, 1.0, 0.0), axis=0, keepdims=True)
            cut = jnp.sum(cut, axis=1, keepdims=True)
            begin_t = jnp.maximum(begin_t, jnp.where(cut <= turn, cut, 0.0))
        mask_t = jnp.where((key_col >= begin_t) & (key_col <= turn), 0.0, NEG)
        loads[5].wait()
        for slot in reversed(range(slots)):
            arrive(slot)
        rebuild(0, slots)
        for g in range(kv):
            write(g, attend_t(g))
        each(slots, drain)
    else:
        row_max[...] = jnp.full(row_max.shape, NEG, jnp.float32)
        total[...] = jnp.zeros(total.shape, jnp.float32)
        loads[5].wait()

        def run(chunk, _):
            for i in range(span):
                arrive(chunk * span + i)
            rebuild(chunk * span, span)
            mask = bias_of(chunk * span, span)
            for g in range(kv):
                row_max[g], total[g] = attend(
                    g, chunk * span, span, mask, row_max[g], total[g]
                )
            return 0

        lax.fori_loop(0, slots // span, run, 0)
        for g in range(kv):
            write(g, total[g])
        each(slots, drain)


def shards(queries, latents, key_up, value_up, documents):
    rows = queries.shape[0]
    kv, rank, width = key_up.shape
    heads = queries.shape[1] // width
    npb, nka = lax.axis_size("pb"), lax.axis_size("ka")
    blocks = npb * nka
    tokens = documents.shape[0]
    back = -(-(tokens // 2 - 1) // rows)
    slots = back + 1
    span = max(d for d in range(1, 9) if slots % d == 0)
    many = slots > 8
    table = jnp.asarray(rotary_tables(rows, blocks, width))
    plan = (rows, blocks, back, span, kv, heads // kv, width, rank, npb, nka)
    bf16, f32 = jnp.bfloat16, jnp.float32
    return pl.pallas_call(
        functools.partial(kernel, plan),
        out_shape=pltpu.VMEM(queries.shape, bf16),
        in_specs=[pl.BlockSpec(memory_space=pltpu.HBM)] * 6,
        out_specs=pl.BlockSpec(memory_space=pltpu.VMEM),
        scratch_shapes=[
            pltpu.VMEM(queries.shape, bf16),
            pltpu.VMEM((rows * kv, 2 * rank), bf16),
            pltpu.VMEM((2, kv, rank, width), bf16),
            pltpu.VMEM((tokens // 128, 128), jnp.int32),
            pltpu.VMEM(table.shape, f32),
            pltpu.VMEM((rows * kv, 2 * rank), bf16),
            pltpu.VMEM((slots, rows * kv, 2 * rank), bf16),
            pltpu.VMEM((slots * rows, width), f32),
            pltpu.VMEM((slots * rows, width), f32),
            pltpu.VMEM((kv, 2 * rank, 2 * width), bf16),
            pltpu.VMEM((kv, slots * rows, width), bf16),
            pltpu.VMEM((kv, slots * rows, 2 * width), bf16),
            pltpu.VMEM((kv, heads // kv * rows if many else 8, 1), f32),
            pltpu.VMEM((kv, heads // kv * rows if many else 8, 2 * width), f32),
            pltpu.SemaphoreType.DMA((6,)),
            pltpu.SemaphoreType.DMA((slots,)),
            pltpu.SemaphoreType.DMA((slots,)),
        ],
        compiler_params=pltpu.CompilerParams(
            collective_id=0, has_side_effects=True, vmem_limit_bytes=63 * 2**20
        ),
    )(
        queries,
        latents.reshape(rows * kv, 2 * rank),
        key_up,
        value_up,
        documents.reshape(tokens // 128, 128),
        table,
    )


def solution(mesh):
    placed = (
        P(("pb", "ka"), "ha"),
        P(("ka", "pb"), "ha", None),
        P("ha", None, None),
        P("ha", None, None),
        P(),
    )
    return jax.shard_map(
        shards, mesh=mesh, in_specs=placed, out_specs=P(("pb", "ka"), "ha"), check_vma=False
    )
```

```python
import functools
import math

import jax
import jax.numpy as jnp
import numpy as np
from jax import lax
from jax.experimental import pallas as pl
from jax.experimental.pallas import tpu as pltpu
from jax.sharding import PartitionSpec as P

NEG = -1e30
MESH = pl.DeviceIdType.MESH


def rotary_tables(rows, blocks, width):
    half = np.arange(width // 2, dtype=np.float64)
    base = 500000.0 ** (-2.0 * half / width)
    wave = 2.0 * np.pi / base
    smooth = (8192.0 / wave - 1.0) / 3.0
    blended = (1.0 - smooth) * base / 8.0 + smooth * base
    freq = np.where(wave < 2048.0, base, np.where(wave > 8192.0, base / 8.0, blended))
    freq = np.concatenate([freq, freq])
    inner = np.arange(rows)[:, None] * freq
    outer = (np.arange(blocks) * rows)[:, None] * freq
    return np.concatenate(
        [np.cos(inner), np.sin(inner), np.cos(outer), np.sin(outer)], axis=0
    ).astype(np.float32)


def split(number, size):
    if size & (size - 1):
        return lax.div(number, size), lax.rem(number, size)
    return lax.shift_right_logical(number, size.bit_length() - 1), number & (size - 1)


def each(count, body):
    if count <= 8:
        for index in range(count):
            body(index)
    else:
        lax.fori_loop(0, count, lambda index, _: (body(index), 0)[1], 0)


def kernel(
    plan,
    q_hbm,
    lat_hbm,
    key_up_hbm,
    value_up_hbm,
    docs_hbm,
    table_hbm,
    out_ref,
    q_buf,
    lat_buf,
    up_buf,
    docs_buf,
    table_buf,
    stage,
    window,
    cosines,
    sines,
    up_all,
    keys,
    values,
    row_max,
    total,
    in_sem,
    send_sem,
    recv_sem,
):
    rows, blocks, back, span, kv, group, width, rank, npb, nka = plan
    slots = back + 1
    pb, ka = lax.axis_index("pb"), lax.axis_index("ka")
    mine_q = pb * nka + ka
    mine_l = ka * npb + pb
    barrier = pltpu.get_barrier_semaphore()

    def greet(slot):
        source = mine_q - back + slot

        @pl.when((source >= 0) & (source != mine_l))
        def _():
            at_ka, at_pb = split(source, npb)
            pl.semaphore_signal(
                barrier, inc=1, device_id={"pb": at_pb, "ka": at_ka}, device_id_type=MESH
            )

    each(slots, greet)

    loads = [
        pltpu.make_async_copy(lat_hbm, lat_buf, in_sem.at[0]),
        pltpu.make_async_copy(key_up_hbm, up_buf.at[0], in_sem.at[1]),
        pltpu.make_async_copy(value_up_hbm, up_buf.at[1], in_sem.at[2]),
        pltpu.make_async_copy(docs_hbm, docs_buf, in_sem.at[3]),
        pltpu.make_async_copy(table_hbm, table_buf, in_sem.at[4]),
        pltpu.make_async_copy(q_hbm, q_buf, in_sem.at[5]),
    ]
    for load in loads:
        load.start()

    def clear(slot):
        @pl.when(mine_q - back + slot < 0)
        def _():
            window[slot] = jnp.zeros(window.shape[1:], window.dtype)

    each(slots, clear)

    loads[0].wait()
    place = lax.broadcasted_iota(jnp.int32, (kv * rows, kv * rows), 0)
    col = lax.broadcasted_iota(jnp.int32, (kv * rows, kv * rows), 1)
    pick = jnp.zeros((kv * rows, kv * rows), jnp.float32)
    for g in range(kv):
        here = (place >= g * rows) & (place < (g + 1) * rows)
        pick = jnp.where(here & (col == (place - g * rows) * kv + g), 1.0, pick)
    stage[...] = jnp.dot(
        pick.astype(jnp.bfloat16), lat_buf[...], preferred_element_type=jnp.float32
    ).astype(jnp.bfloat16)

    def keep(step):
        @pl.when(mine_l + step == mine_q)
        def _():
            window[back - step] = stage[...]

    each(slots, keep)

    last = jnp.minimum(blocks - 1, mine_l + back)
    own = ((mine_q >= mine_l) & (mine_q <= last)).astype(jnp.int32)
    partners = last - mine_l + 1 - own

    @pl.when(partners > 0)
    def _():
        pl.semaphore_wait(barrier, partners)

    def copy_to(step):
        at_pb, at_ka = split(mine_l + step, nka)
        return pltpu.make_async_remote_copy(
            src_ref=stage,
            dst_ref=window.at[back - step],
            send_sem=send_sem.at[step],
            recv_sem=recv_sem.at[back - step],
            device_id={"pb": at_pb, "ka": at_ka},
            device_id_type=MESH,
        )

    def send(step):
        target = mine_l + step

        @pl.when((target < blocks) & (target != mine_q))
        def _():
            copy_to(step).start()

    each(slots, send)

    loads[1].wait()
    loads[2].wait()
    up_all[...] = jnp.zeros(up_all.shape, up_all.dtype)
    for g in range(kv):
        up_all[g, :rank, :width] = up_buf[0, g]
        up_all[g, rank:, width:] = up_buf[1, g]
    loads[3].wait()
    docs = docs_buf[...]
    query_at = mine_q * rows + lax.broadcasted_iota(jnp.int32, (rows, 1), 0)
    query_at = query_at.astype(jnp.float32)
    begin = jnp.zeros((rows, 1), jnp.float32)
    for doc in range(3):
        cut = jnp.sum(jnp.where(docs <= doc, 1.0, 0.0), axis=0, keepdims=True)
        cut = jnp.sum(cut, axis=1, keepdims=True)
        begin = jnp.maximum(begin, jnp.where(cut <= query_at, cut, 0.0))

    loads[4].wait()
    cos_row, sin_row = table_buf[:rows], table_buf[rows : 2 * rows]
    lane = lax.broadcasted_iota(jnp.int32, (1, width), 1)
    sign = jnp.where(lane < width // 2, -1.0, 1.0)

    def row_of(slot):
        return slot * rows if isinstance(slot, int) else pl.multiple_of(slot * rows, rows)

    def angles(slot):
        first = jnp.maximum(mine_q - back + slot, 0)
        cos_block = table_buf[pl.ds(2 * rows + first, 1)]
        sin_block = table_buf[pl.ds(2 * rows + blocks + first, 1)]
        cosines[pl.ds(row_of(slot), rows)] = cos_row * cos_block - sin_row * sin_block
        sines[pl.ds(row_of(slot), rows)] = (sin_row * cos_block + cos_row * sin_block) * sign

    each(slots, angles)
    values[:, :, width:] = jnp.ones((kv, slots * rows, width), jnp.bfloat16)

    def bias_of(first, count):
        key_at = (mine_q - back + first) * rows
        key_at = key_at + lax.broadcasted_iota(jnp.int32, (1, count * rows), 1)
        key_at = key_at.astype(jnp.float32)
        return jnp.where((key_at >= begin) & (key_at <= query_at), 0.0, NEG)

    def arrive(slot):
        source = mine_q - back + slot

        @pl.when((source >= 0) & (source != mine_l))
        def _():
            pltpu.make_async_copy(stage, window.at[slot], recv_sem.at[slot]).wait()

    def rebuild(first, count):
        at, reach = row_of(first), count * rows
        for g in range(kv):
            latents = [window[first + i, g * rows : (g + 1) * rows] for i in range(count)]
            both = jnp.dot(
                jnp.concatenate(latents), up_all[g], preferred_element_type=jnp.float32
            )
            key = both[:, :width] * cosines[pl.ds(at, reach)]
            key = key + pltpu.roll(both[:, :width], width // 2, 1) * sines[pl.ds(at, reach)]
            keys[g, pl.ds(at, reach)] = key.astype(jnp.bfloat16)
            values[g, pl.ds(at, reach), :width] = both[:, width:].astype(jnp.bfloat16)

    factor = math.log2(math.e) * width ** (-0.5)

    def attend(g, first, count, bias, before, sums):
        at, reach = row_of(first), count * rows
        heads = range(g * group, (g + 1) * group)
        stacked = jnp.concatenate([q_buf[:, h * width : (h + 1) * width] for h in heads])
        scores = lax.dot_general(
            stacked,
            keys[g, pl.ds(at, reach)],
            (((1,), (1,)), ((), ())),
            preferred_element_type=jnp.float32,
        )
        scores = scores + jnp.concatenate([bias] * group)
        top = jnp.max(scores, axis=1, keepdims=True)
        if before is not None:
            top = jnp.maximum(top, before)
        weights = jnp.exp2((scores - top) * factor).astype(jnp.bfloat16)
        part = jnp.dot(weights, values[g, pl.ds(at, reach)], preferred_element_type=jnp.float32)
        if before is not None:
            part = part + sums * jnp.exp2((before - top) * factor)
        return top, part

    def score_t(g, first, count, mask_t):
        heads = range(g * group, (g + 1) * group)
        stacked = jnp.concatenate([q_buf[:, h * width : (h + 1) * width] for h in heads])
        at, reach = first * rows, count * rows
        scores = lax.dot_general(
            keys[g, at : at + reach],
            stacked,
            (((1,), (1,)), ((), ())),
            preferred_element_type=jnp.float32,
        )
        return scores + mask_t[at : at + reach]

    def attend_t(g, scores):
        top = jnp.max(scores, axis=0, keepdims=True)
        weights = jnp.exp2((scores - top) * factor).astype(jnp.bfloat16)
        return lax.dot_general(
            weights, values[g], (((0,), (0,)), ((), ())), preferred_element_type=jnp.float32
        )

    def write(g, part):
        ratio = (part[:, :width] / part[:, width:]).astype(jnp.bfloat16)
        for i in range(group):
            h = g * group + i
            out_ref[:, h * width : (h + 1) * width] = ratio[i * rows : (i + 1) * rows]

    def drain(step):
        target = mine_l + step

        @pl.when((target < blocks) & (target != mine_q))
        def _():
            copy_to(step).wait_send()

    if slots <= 8:
        key_col = (mine_q - back) * rows + lax.broadcasted_iota(jnp.int32, (slots * rows, 1), 0)
        key_col = key_col.astype(jnp.float32)
        q_lane = lax.broadcasted_iota(jnp.int32, (1, group * rows), 1)
        turn = q_lane
        for i in range(1, group):
            turn = jnp.where(q_lane >= i * rows, q_lane - i * rows, turn)
        turn = (mine_q * rows + turn).astype(jnp.float32)
        begin_t = jnp.zeros((1, group * rows), jnp.float32)
        for doc in range(3):
            cut = jnp.sum(jnp.where(docs <= doc, 1.0, 0.0), axis=0, keepdims=True)
            cut = jnp.sum(cut, axis=1, keepdims=True)
            begin_t = jnp.maximum(begin_t, jnp.where(cut <= turn, cut, 0.0))
        mask_t = jnp.where((key_col >= begin_t) & (key_col <= turn), 0.0, NEG)
        loads[5].wait()
        for slot in reversed(range(1, slots)):
            arrive(slot)
        rebuild(1, slots - 1)
        nearer = [score_t(g, 1, slots - 1, mask_t) for g in range(kv)]
        arrive(0)
        rebuild(0, 1)
        for g in range(kv):
            write(g, attend_t(g, jnp.concatenate([score_t(g, 0, 1, mask_t), nearer[g]])))
        each(slots, drain)
    else:
        row_max[...] = jnp.full(row_max.shape, NEG, jnp.float32)
        total[...] = jnp.zeros(total.shape, jnp.float32)
        loads[5].wait()

        def run(chunk, _):
            for i in range(span):
                arrive(chunk * span + i)
            rebuild(chunk * span, span)
            mask = bias_of(chunk * span, span)
            for g in range(kv):
                row_max[g], total[g] = attend(
                    g, chunk * span, span, mask, row_max[g], total[g]
                )
            return 0

        lax.fori_loop(0, slots // span, run, 0)
        for g in range(kv):
            write(g, total[g])
        each(slots, drain)


def shards(queries, latents, key_up, value_up, documents):
    rows = queries.shape[0]
    kv, rank, width = key_up.shape
    heads = queries.shape[1] // width
    npb, nka = lax.axis_size("pb"), lax.axis_size("ka")
    blocks = npb * nka
    tokens = documents.shape[0]
    back = -(-(tokens // 2 - 1) // rows)
    slots = back + 1
    span = max(d for d in range(1, 9) if slots % d == 0)
    many = slots > 8
    table = jnp.asarray(rotary_tables(rows, blocks, width))
    plan = (rows, blocks, back, span, kv, heads // kv, width, rank, npb, nka)
    bf16, f32 = jnp.bfloat16, jnp.float32
    return pl.pallas_call(
        functools.partial(kernel, plan),
        out_shape=pltpu.VMEM(queries.shape, bf16),
        in_specs=[pl.BlockSpec(memory_space=pltpu.HBM)] * 6,
        out_specs=pl.BlockSpec(memory_space=pltpu.VMEM),
        scratch_shapes=[
            pltpu.VMEM(queries.shape, bf16),
            pltpu.VMEM((rows * kv, 2 * rank), bf16),
            pltpu.VMEM((2, kv, rank, width), bf16),
            pltpu.VMEM((tokens // 128, 128), jnp.int32),
            pltpu.VMEM(table.shape, f32),
            pltpu.VMEM((rows * kv, 2 * rank), bf16),
            pltpu.VMEM((slots, rows * kv, 2 * rank), bf16),
            pltpu.VMEM((slots * rows, width), f32),
            pltpu.VMEM((slots * rows, width), f32),
            pltpu.VMEM((kv, 2 * rank, 2 * width), bf16),
            pltpu.VMEM((kv, slots * rows, width), bf16),
            pltpu.VMEM((kv, slots * rows, 2 * width), bf16),
            pltpu.VMEM((kv, heads // kv * rows if many else 8, 1), f32),
            pltpu.VMEM((kv, heads // kv * rows if many else 8, 2 * width), f32),
            pltpu.SemaphoreType.DMA((6,)),
            pltpu.SemaphoreType.DMA((slots,)),
            pltpu.SemaphoreType.DMA((slots,)),
        ],
        compiler_params=pltpu.CompilerParams(
            collective_id=0, has_side_effects=True, vmem_limit_bytes=63 * 2**20
        ),
    )(
        queries,
        latents.reshape(rows * kv, 2 * rank),
        key_up,
        value_up,
        documents.reshape(tokens // 128, 128),
        table,
    )


def solution(mesh):
    placed = (
        P(("pb", "ka"), "ha"),
        P(("ka", "pb"), "ha", None),
        P("ha", None, None),
        P("ha", None, None),
        P(),
    )
    return jax.shard_map(
        shards, mesh=mesh, in_specs=placed, out_specs=P(("pb", "ka"), "ha"), check_vma=False
    )
```
